32 devices in a mesh: groups: 2 (over y), ctx: 4 (over z), mp: 4 (over x, core).
Axes of the slice: x: 2, y: 2, z: 4, core: 2. Of those that a mesh axis runs over, the one named last changes fastest.
Arguments:
- features: bfloat16 [4, 512, 1536], P('groups', 'ctx'), parts along dimension 0, may hold values from -6 to 6
- frame_counts: int32 [4], P('groups'), parts along dimension 0, may hold values from 1 to 512, 768 in all
- attn_gain: float32 [1536], replicated, may hold values from 0.25 to 1.75
- w_qkv: bfloat16 [3, 1536, 1024], P(None, None, 'mp'), may hold values from -2 to 2
- w_out: bfloat16 [1024, 1536], P('mp'), may hold values from -0.375 to 0.375
- conv_gain: float32 [1536], replicated, may hold values from 0.25 to 1.75
- w_glu: bfloat16 [2, 1536, 1536], P(None, None, 'mp'), may hold values from -0.15625 to 0.15625
- kernel: float32 [31, 1536], P(None, 'mp'), may hold values from -2 to 2
- bn_scale: float32 [1536], P('mp'), may hold values from 0.5 to 2
- bn_shift: float32 [1536], P('mp'), may hold values from -2.5 to 2.5
- w_pw: bfloat16 [1536, 1536], P('mp'), may hold values from -0.15625 to 0.15625
- clip_level: int32 [1536], replicated, may hold values from 6 to 39
Outputs:
- encoded: bfloat16 [4, 512, 1536], P('groups', ('ctx', 'mp')), parts along dimension 0
The draws below stay inside these ranges and needn't reach their ends.
There are 2 independent parts, one for each index of `groups`. The reference program is written for one: setup_inputs(seed, part) draws one part's arguments, and reference() takes and returns one part's arrays. A program takes and returns all parts, laid end to end along the dimension named above; an argument that names none is the same for every part. Nothing has to cross between parts.
Inputs may be any that keep to these rules, and one draw needn't show every extreme that they name: frame_counts[s] frames of recording s fill slots 0 to frame_counts[s] - 1, later slots are padding; some recording fills all 512 slots.
All inputs are finite; a program needn't handle non-finite values.
Results may differ from the reference program's by a relative error of at most 0.023.
Values may be sent and summed in bfloat16 or wider, within the bound.
A program may use at most 128 MiB of HBM per device.

```python
import math
import jax
import jax.numpy as jnp
import numpy as np
from jax import lax

D = 1536
HEADS = 16
HEAD_DIM = 64
KERNEL = 31
SEQS = 2
LENGTH = 512
N_MP = 4


def draw_w_qkv(key, part):
    columns = HEADS * HEAD_DIM
    sub_keys = jax.random.split(key, 1)
    base = jax.random.normal(sub_keys[0], (3, D, columns), jnp.float32) / math.sqrt(D)
    drawn = base * jnp.array([2.0, 2.0, 1.0], jnp.float32)[:, None, None]
    return jnp.clip(drawn, -2.0, 2.0).astype(jnp.bfloat16)


def plant(values, stream_key, least, top_value):
    shape = values.shape
    spot = [jax.random.randint(jax.random.fold_in(stream_key, axis), (), 0, shape[axis]) for axis in range(len(shape))]
    values = values.at[tuple(spot)].set(least)
    longest = shape.index(max(shape))
    spot[longest] = (spot[longest] + 1) % shape[longest]
    return values.at[tuple(spot)].set(top_value)


def block_scale(stream_key, extent, cuts, smallest, high):
    level = 1.0
    for position, parts in cuts:
        draws = jax.random.uniform(jax.random.fold_in(jax.random.fold_in(stream_key, 6), position), (parts,), jnp.float32, smallest / len(cuts), high / len(cuts))
        level = level * jnp.repeat(jnp.exp(draws), extent[position] // parts).reshape((-1,) + (1,) * (len(extent) - 1 - position))
    return level


def profile(amount, total, reach, lean):
    weights = [(1 << 20) // math.isqrt(standing ** lean) + 1 for standing in range(2, amount + 1)]
    surplus, given = total - reach - (amount - 1), [1] * (amount - 1)
    while surplus > 0:
        free = [i for i in range(amount - 1) if given[i] < reach]
        mass, budget = sum([weights[i] for i in free]), surplus
        for i in free:
            addition = min(reach - given[i], max(1, budget * weights[i] // mass), surplus)
            given[i] = given[i] + addition
            surplus = surplus - addition
    return np.array([reach] + given)


def uneven_parts(stream_key, count, total, limit, skew):
    if count == 2:
        one = jax.random.randint(stream_key, (), max(1, total - limit), min(limit, total - 1) + 1)
        return jnp.stack([one, total - one])
    sizes = jnp.asarray(profile(count, total, limit, skew), jnp.int32)
    couples = (count - 1) // 2
    giver, sink = sizes[1:1 + 2 * couples:2], sizes[2:2 + 2 * couples:2]
    margin = jnp.minimum(giver - 1, limit - sink)
    passed = jax.random.randint(jax.random.fold_in(stream_key, 1), (couples,), 0, 1 << 20) % (margin + 1)
    sizes = sizes.at[1:1 + 2 * couples:2].set(giver - passed).at[2:2 + 2 * couples:2].set(sink + passed)
    return sizes[jax.random.permutation(jax.random.fold_in(stream_key, 2), count)]


def bell_draw(stream_key, shape, scale, reach, cuts=(), kind=jnp.bfloat16):
    values = scale * jax.random.normal(stream_key, shape, jnp.float32)
    if cuts:
        values = values * block_scale(stream_key, shape, cuts, -0.22, 0.18)
    return jnp.clip(values, -reach, reach).astype(kind)


def setup_inputs(seed: int = 0, part: int = 0) -> dict:
    keys = jax.random.split(jax.random.key(seed), 13)
    part_keys = jax.random.split(jax.random.fold_in(keys[12], part), 13)
    features = bell_draw(part_keys[0], (SEQS, LENGTH, D), 1.0, 6.0, ((1, 4),))
    frame_counts = uneven_parts(part_keys[1], SEQS, 3 * SEQS * LENGTH // 4, LENGTH, 2).astype(jnp.int32)
    attn_gain = jnp.clip(1.0 + 0.15 * jax.random.normal(keys[2], (D,), jnp.float32), 0.25, 1.75)
    w_qkv = draw_w_qkv(jax.random.fold_in(keys[12], 71), part)
    w_out = bell_draw(keys[4], (HEADS * HEAD_DIM, D), (HEADS * HEAD_DIM // 4) ** -0.5, 0.375, ((0, 4),))
    conv_gain = jnp.clip(1.0 + 0.15 * jax.random.normal(keys[5], (D,), jnp.float32), 0.25, 1.75)
    w_glu = bell_draw(keys[6], (2, D, D), D ** -0.5, 0.15625, ((2, 4),))
    kernel = bell_draw(keys[7], (KERNEL, D), (KERNEL // 4) ** -0.5, 2.0, ((1, 4),), jnp.float32)
    bn_scale = jnp.clip(jnp.exp(math.log(2.0) - 1.3862944 * jax.random.uniform(keys[8], (D,), jnp.float32) ** block_scale(keys[8], (D,), ((0, 4),), -0.2, 0.2)), 0.5, 2.0)
    bn_shift = bell_draw(keys[9], (D,), 0.5, 2.5, ((0, 4),), jnp.float32)
    w_pw = bell_draw(keys[10], (D, D), D ** -0.5, 0.15625, ((0, 4),))
    clip_level = plant(jax.random.randint(keys[11], (D,), 6, 40), jax.random.fold_in(keys[11], 1), 6, 39).astype(jnp.int32)
    return {"features": features, "frame_counts": frame_counts, "attn_gain": attn_gain, "w_qkv": w_qkv, "w_out": w_out, "conv_gain": conv_gain, "w_glu": w_glu, "kernel": kernel, "bn_scale": bn_scale, "bn_shift": bn_shift, "w_pw": w_pw, "clip_level": clip_level}


epsilon = 1e-05
masked_score = -1e+30

def layer_norm(values, gain):
    centre = lax.optimization_barrier(jnp.mean(values, axis=-1, keepdims=True))
    centred = values - centre
    variance = lax.optimization_barrier(jnp.mean(centred * centred, axis=-1, keepdims=True))
    return centred * lax.rsqrt(variance + epsilon) * gain

def grouped_sum(row_operand, weight_rows):
    group_width = row_operand.shape[1] // N_MP
    total_sum = jnp.zeros((row_operand.shape[0], weight_rows.shape[1]), jnp.float32)
    for group_index in range(N_MP):
        lower = group_index * group_width
        group_term = jnp.dot(row_operand[:, lower:lower + group_width], weight_rows[lower:lower + group_width], preferred_element_type=jnp.float32)
        total_sum = total_sum + lax.optimization_barrier(group_term.astype(jnp.bfloat16)).astype(jnp.float32)
    return total_sum

def reference(features, frame_counts, attn_gain, w_qkv, w_out, conv_gain, w_glu, kernel, bn_scale, bn_shift, w_pw, clip_level):
    records, length, model_width = features.shape
    flat_rows = records * length
    normed = layer_norm(features.astype(jnp.float32), attn_gain).astype(jnp.bfloat16).reshape(flat_rows, model_width)
    stacked = []
    for slot_index in range(3):
        projected = jnp.dot(normed, w_qkv[slot_index], preferred_element_type=jnp.float32).astype(jnp.bfloat16)
        stacked.append(lax.optimization_barrier(projected).astype(jnp.float32).reshape(records, length, HEADS, HEAD_DIM))
    positions = jnp.arange(length, dtype=jnp.int32)

    def attend(record_item):
        queries, key_rows, value_rows, limit_here = record_item
        scores = jnp.einsum('qhe,khe->hqk', queries, key_rows) * HEAD_DIM ** (-0.5)
        scores = jnp.where((positions < limit_here)[None, None, :], scores, masked_score)
        row_max = lax.optimization_barrier(jnp.max(scores, axis=-1, keepdims=True))
        weights = jnp.exp(scores - row_max)
        row_sum = lax.optimization_barrier(jnp.sum(weights, axis=-1))
        rounded = lax.optimization_barrier(weights.astype(jnp.bfloat16)).astype(jnp.float32)
        mixture = jnp.einsum('hqk,khe->qhe', rounded, value_rows) / jnp.transpose(row_sum)[:, :, None]
        return mixture.astype(jnp.bfloat16).reshape(length, HEADS * HEAD_DIM)
    attended = lax.map(attend, (stacked[0], stacked[1], stacked[2], frame_counts)).reshape(flat_rows, HEADS * HEAD_DIM)
    residual = features.astype(jnp.float32).reshape(flat_rows, model_width) + grouped_sum(attended, w_out)
    normed_conv = layer_norm(residual, conv_gain).astype(jnp.bfloat16)
    value_half = jnp.dot(normed_conv, w_glu[0], preferred_element_type=jnp.float32)
    gate_half = jnp.dot(normed_conv, w_glu[1], preferred_element_type=jnp.float32)
    gated_rows = (value_half * jax.nn.sigmoid(gate_half)).astype(jnp.bfloat16).reshape(records, length, model_width)
    frame_live = positions[None, :] < frame_counts[:, None]
    gated_rows = jnp.where(frame_live[..., None], gated_rows, jnp.zeros((), jnp.bfloat16))
    rim_width = KERNEL // 2
    padded = jnp.pad(lax.optimization_barrier(gated_rows), ((0, 0), (rim_width, rim_width), (0, 0)))
    depthwise = jnp.zeros((records, length, model_width), jnp.float32)
    for tap_index in range(KERNEL):
        depthwise = depthwise + padded[:, tap_index:tap_index + length, :].astype(jnp.float32) * kernel[tap_index]
    activated = jax.nn.silu(depthwise * bn_scale + bn_shift).astype(jnp.bfloat16).reshape(flat_rows, model_width)
    combined = residual + grouped_sum(activated, w_pw)
    clip_bound = clip_level.astype(jnp.float32) / 16.0
    clipped = jnp.clip(combined, -clip_bound, clip_bound).reshape(records, length, model_width)
    return jnp.where(frame_live[..., None], clipped, 0.0).astype(jnp.bfloat16)
```

```python
import functools

import jax
import jax.numpy as jnp
from jax import lax
from jax.experimental import pallas as pl
from jax.experimental.pallas import tpu as pltpu
from jax.sharding import PartitionSpec as P

MESH = pl.DeviceIdType.MESH
HEAD_DIM = 64
LANES = 128
RIM = 16
epsilon = 1e-05
masked_score = -1e30
f32 = jnp.float32
bf16 = jnp.bfloat16


def loop(count, step):
    if count <= 2:
        for i in range(count):
            step(i)
    else:
        lax.fori_loop(0, count, lambda i, carry: (step(i), carry)[1], 0)


def when(cond):
    if cond is True:
        return lambda f: f()
    return lambda f: pl.when(cond)(lambda: f())


def normalise(values, gain):
    centred = values - jnp.mean(values, axis=-1, keepdims=True)
    variance = jnp.mean(centred * centred, axis=-1, keepdims=True)
    return (centred * lax.rsqrt(variance + epsilon) * gain).astype(bf16)


def fused(
    n, nx, recs, frames, taps, cols,
    feat, counts, ag, wqkv_h, wout_h, cg, wglu_h, ker, bns, bnb, wpw_h, clip, out,
    wqkv, wo, wglu, wpw, xn, qkv_s, qkv_r, atto, att_all, parts, sibs, res, gb, gp, halo, act,
    p5, s5, sum5, x5,
    ld, qs, qr, wos, wor, zs, zr, fs, fr, ss, sr, hs, hr, bs, br, es, er,
):
    c = lax.axis_index("ctx")
    m = lax.axis_index("mp")
    x = lax.div(m, 2)
    core = lax.rem(m, 2)
    sibling = {"mp": x * 2 + (1 - core)}
    rows, width = feat.shape
    pairs = wqkv.shape[2] // LANES
    units = recs * pairs
    chans = gb.shape[2]
    rm = frames // (2 * nx)
    slabs = width // cols
    group = min(recs, 2)
    block = group * frames

    def ctx_at(k):
        return lax.rem(c + k, n)

    def has_unit(rank):
        return True if units == n else rank < units

    def x_peer(k):
        return {"mp": lax.rem(x + k, nx) * 2 + core}

    def remote(src, dst, send, recv, where):
        return pltpu.make_async_remote_copy(
            src_ref=src, dst_ref=dst, send_sem=send, recv_sem=recv, device_id=where, device_id_type=MESH
        )

    loads = [pltpu.make_async_copy(wqkv_h.at[i], wqkv.at[i], ld.at[i]) for i in range(3)]
    loads.append(pltpu.make_async_copy(wglu_h, wglu, ld.at[3]))
    loads.append(pltpu.make_async_copy(wpw_h, wpw, ld.at[4]))
    loads.append(pltpu.make_async_copy(wout_h, wo.at[x], ld.at[5]))
    for i in (1, 0, 2, 5, 3, 4):
        loads[i].start()

    barrier = pltpu.get_barrier_semaphore()
    for k in range(1, n):
        pl.semaphore_signal(barrier, inc=1, device_id={"ctx": ctx_at(k)}, device_id_type=MESH)
    for k in range(1, nx):
        pl.semaphore_signal(barrier, inc=1, device_id=x_peer(k), device_id_type=MESH)
    pl.semaphore_signal(barrier, inc=1, device_id=sibling, device_id_type=MESH)

    gain = ag[...].reshape(1, width)

    def norm_in(i):
        at = pl.ds(pl.multiple_of(i * 32, 32), 32)
        xn[at, :] = normalise(feat[at, :].astype(f32), gain)

    lax.fori_loop(0, rows // 32, lambda i, carry: (norm_in(i), carry)[1], 0)

    pl.semaphore_wait(barrier, n - 1 + nx - 1 + 1)

    w_copies = []
    for k in range(1, nx):
        w_copies.append(remote(wout_h, wo.at[x], wos.at[k], wor.at[k], x_peer(k)))
        w_copies[-1].start()

    q_copies = []
    for i in (1, 0, 2):
        loads[i].wait()

        def project(g, i=i):
            at = pl.ds(pl.multiple_of(g * block, block), block)
            made = jnp.dot(xn[at, :], wqkv[i], preferred_element_type=f32).astype(bf16)
            for r in range(group):
                for p in range(pairs):
                    piece = made[r * frames : (r + 1) * frames, p * LANES : (p + 1) * LANES]
                    qkv_s[(g * group + r) * pairs + p, i] = piece

        loop(recs // group, project)
        for k in range(1, n):
            dest = ctx_at(k)
            copy = remote(
                qkv_s.at[lax.rem(dest, units), i], qkv_r.at[c, i], qs.at[i, k], qr.at[i, k], {"ctx": dest}
            )
            when(has_unit(dest))(copy.start)
            q_copies.append((copy, dest))

        @when(has_unit(c))
        def _(i=i):
            qkv_r[c, i] = qkv_s[lax.rem(c, units), i]

    z_copies = [
        remote(atto.at[k], att_all.at[x, lax.rem(c, units)], zs.at[k], zr.at[k], {"ctx": ctx_at(k)})
        for k in range(1, n)
    ]

    @when(has_unit(c))
    def _():
        for copy, _dest in q_copies:
            copy.wait_recv()
    own_rec = lax.div(lax.rem(c, units), pairs)
    live_keys = counts[own_rec]
    key_count = n * frames
    lane = lax.broadcasted_iota(jnp.int32, (1, LANES), 1)
    low = lane < HEAD_DIM
    seen = lax.broadcasted_iota(jnp.int32, (1, key_count), 1) < live_keys

    def attend(k0):
        keys = qkv_r[:, 1].reshape(key_count, LANES)
        values = qkv_r[:, 2].reshape(key_count, LANES)
        queries = jnp.concatenate([qkv_r[ctx_at(k0), 0], qkv_r[ctx_at(k0 + 1), 0]], axis=0)
        heads = []
        for h in range(2):
            mine = jnp.where(low if h == 0 else jnp.logical_not(low), queries, jnp.zeros((), bf16))
            scores = lax.dot_general(
                mine, keys, (((1,), (1,)), ((), ())), preferred_element_type=f32
            ) * (HEAD_DIM**-0.5)
            scores = jnp.where(seen, scores, masked_score)
            weights = jnp.exp(scores - jnp.max(scores, axis=-1, keepdims=True))
            total = jnp.sum(weights, axis=-1, keepdims=True)
            mixed = jnp.dot(weights.astype(bf16), values, preferred_element_type=f32)
            heads.append(mixed / total)
        both = jnp.where(low, heads[0], heads[1]).astype(bf16)
        atto[k0] = both[:frames]
        atto[k0 + 1] = both[frames:]

    def give(k):
        if k == 0:
            att_all[x, lax.rem(c, units)] = atto[0]
        else:
            z_copies[k - 1].start()

    @when(has_unit(c))
    def _():
        if n <= 4:
            for k0 in range(0, n, 2):
                attend(k0)
                give(k0)
                give(k0 + 1)
        else:
            lax.fori_loop(0, n // 2, lambda i, carry: (attend(2 * i), carry)[1], 0)
            for k in range(n):
                give(k)

    f_copies = []
    for k in range(n):
        unit = lax.rem(c - k + n, n)
        spot = lax.rem(unit, units)

        @when(has_unit(unit))
        def _(k=k, unit=unit, spot=spot):
            if k > 0:
                remote(atto.at[k], att_all.at[x, spot], zs.at[k], zr.at[k], {"ctx": unit}).wait_recv()
            for j in range(1, nx):
                remote(
                    att_all.at[x, spot], att_all.at[x, spot], fs.at[j, k], fr.at[j, k], x_peer(j)
                ).start()

        for j in range(1, nx):
            f_copies.append(
                (remote(att_all.at[x, spot], att_all.at[x, spot], fs.at[j, k], fr.at[j, k], x_peer(j)), unit)
            )

    loads[5].wait()
    for copy in w_copies:
        copy.wait_recv()
    for copy, unit in f_copies:
        when(has_unit(unit))(copy.wait_recv)

    s_copies = []
    stacked_w = nx * pairs * LANES
    for j in range(slabs):
        def partial(g, j=j):
            gathered = jnp.concatenate(
                [
                    jnp.concatenate(
                        [att_all[i, (g * group + r) * pairs + p] for i in range(nx) for p in range(pairs)],
                        axis=1,
                    )
                    for r in range(group)
                ],
                axis=0,
            )
            weight = wo[:, :, j * cols : (j + 1) * cols].reshape(stacked_w, cols)
            at = pl.ds(pl.multiple_of(g * block, block), block)
            parts[j, at, :] = jnp.dot(gathered, weight, preferred_element_type=f32).astype(bf16)

        loop(recs // group, partial)
        copy = remote(parts.at[j], sibs.at[j], ss.at[j], sr.at[j], sibling)
        copy.start()
        s_copies.append(copy)
    for copy in s_copies:
        copy.wait_recv()

    conv_gain = cg[...].reshape(1, width)

    def norm_conv(i):
        at = pl.ds(pl.multiple_of(i * 32, 32), 32)
        added = jnp.concatenate(
            [parts[j, at, :].astype(f32) + sibs[j, at, :].astype(f32) for j in range(slabs)], axis=1
        )
        total = feat[at, :].astype(f32) + added
        res[at, :] = total
        xn[at, :] = normalise(total, conv_gain)

    lax.fori_loop(0, rows // 32, lambda i, carry: (norm_conv(i), carry)[1], 0)

    loads[3].wait()
    first_frame = c * frames
    frame_ids = first_frame + lax.broadcasted_iota(jnp.int32, (frames, 1), 0)

    def gate(g):
        at = pl.ds(pl.multiple_of(g * block, block), block)
        value_half = jnp.dot(xn[at, :], wglu[0], preferred_element_type=f32)
        gate_half = jnp.dot(xn[at, :], wglu[1], preferred_element_type=f32)
        gated = value_half * jax.nn.sigmoid(gate_half)
        for r in range(group):
            rec = g * group + r
            kept = jnp.where(frame_ids < counts[rec], gated[r * frames : (r + 1) * frames], 0.0).astype(bf16)
            gb[rec] = kept
            gp[rec, RIM : RIM + frames, :] = kept.astype(f32)

    loop(recs // group, gate)

    def up():
        return remote(gb.at[:, frames - RIM : frames, :], halo.at[0], hs.at[0], hr.at[0], {"ctx": lax.rem(c + 1, n)})

    def down():
        return remote(gb.at[:, 0:RIM, :], halo.at[1], hs.at[1], hr.at[1], {"ctx": lax.rem(c + n - 1, n)})

    @pl.when(c < n - 1)
    def _():
        up().start()

    @pl.when(c > 0)
    def _():
        down().start()

    scale = bns[...].reshape(1, chans)
    shift = bnb[...].reshape(1, chans)

    def depthwise(rec, start, count):
        for lo in range(0, chans, LANES):
            hi = min(lo + LANES, chans)
            total = jnp.zeros((count, hi - lo), f32)
            for tap in range(taps):
                begin = start + tap + RIM - taps // 2
                total = total + gp[rec, begin : begin + count, lo:hi] * ker[tap : tap + 1, lo:hi]
            v = total * scale[:, lo:hi] + shift[:, lo:hi]
            act[rec, start : start + count, lo:hi] = (v * jax.nn.sigmoid(v)).astype(bf16)

    loop(recs, lambda rec: depthwise(rec, RIM, frames - 2 * RIM))

    @pl.when(c > 0)
    def _():
        up().wait_recv()

    @pl.when(c == 0)
    def _():
        halo[0] = jnp.zeros(halo.shape[1:], bf16)

    @pl.when(c < n - 1)
    def _():
        down().wait_recv()

    @pl.when(c == n - 1)
    def _():
        halo[1] = jnp.zeros(halo.shape[1:], bf16)

    def edges(rec):
        gp[rec, 0:RIM, :] = halo[0, rec].astype(f32)
        gp[rec, RIM + frames : 2 * RIM + frames, :] = halo[1, rec].astype(f32)
        depthwise(rec, 0, RIM)
        depthwise(rec, frames - RIM, RIM)

    loop(recs, edges)

    loads[4].wait()
    b_copies = []
    for j in range(slabs):
        def pointwise(g, j=j):
            at = pl.ds(g * group, group)
            made = jnp.dot(
                act[at].reshape(block, chans), wpw[:, j * cols : (j + 1) * cols], preferred_element_type=f32
            )
            p5[j, at] = made.reshape(group, nx, 2, rm, cols).astype(bf16)

        loop(recs // group, pointwise)
        copy = remote(p5.at[j, :, :, 1 - core], s5.at[j], bs.at[j], br.at[j], sibling)
        copy.start()
        b_copies.append(copy)

    e_copies = []
    for j in range(slabs):
        b_copies[j].wait_recv()
        for i in range(nx):
            sum5[j, i] = (p5[j, :, i, core].astype(f32) + s5[j, :, i].astype(f32)).astype(bf16)
        for k in range(1, nx):
            copy = remote(sum5.at[j, lax.rem(x + k, nx)], x5.at[j, k], es.at[j, k], er.at[j, k], x_peer(k))
            copy.start()
            e_copies.append(copy)

    row_start = pl.multiple_of(m * rm, rm)
    mine_ids = first_frame + row_start + lax.broadcasted_iota(jnp.int32, (rm, 1), 0)
    bound = clip[...].reshape(1, width).astype(f32) / 16.0
    e_at = 0
    for j in range(slabs):
        for k in range(1, nx):
            e_copies[e_at].wait_recv()
            e_at += 1
        limit = bound[:, j * cols : (j + 1) * cols]

        def finish(rec, j=j, limit=limit):
            at = pl.ds(pl.multiple_of(rec * frames + row_start, rm), rm)
            total = res[at, j * cols : (j + 1) * cols] + sum5[j, x, rec].astype(f32)
            for k in range(1, nx):
                total = total + x5[j, k, rec].astype(f32)
            clipped = jnp.minimum(jnp.maximum(total, -limit), limit)
            out[rec, :, j * cols : (j + 1) * cols] = jnp.where(mine_ids < counts[rec], clipped, 0.0).astype(bf16)

        loop(recs, finish)

    for copy, dest in q_copies:
        when(has_unit(dest))(copy.wait_send)

    @when(has_unit(c))
    def _():
        for copy in z_copies:
            copy.wait_send()

    for copy, unit in f_copies:
        when(has_unit(unit))(copy.wait_send)
    for copy in w_copies + s_copies + b_copies + e_copies:
        copy.wait_send()

    @pl.when(c < n - 1)
    def _():
        up().wait_send()

    @pl.when(c > 0)
    def _():
        down().wait_send()


def shards(n, mp, features, frame_counts, attn_gain, w_qkv, w_out, conv_gain, w_glu, kernel, bn_scale, bn_shift, w_pw, clip_level):
    recs, frames, width = features.shape
    nx = mp // 2
    rows = recs * frames
    cols = width // 2
    slabs = 2
    local = w_qkv.shape[2]
    units = recs * local // LANES
    chans = w_glu.shape[2]
    rm = frames // mp
    taps = kernel.shape[0]
    vmem = pl.BlockSpec(memory_space=pltpu.VMEM)
    hbm = pl.BlockSpec(memory_space=pl.ANY)
    dma = pltpu.SemaphoreType.DMA
    scratch = [
        pltpu.VMEM(w_qkv.shape, bf16),
        pltpu.VMEM((nx, local, width), bf16),
        pltpu.VMEM(w_glu.shape, bf16),
        pltpu.VMEM(w_pw.shape, bf16),
        pltpu.VMEM((rows, width), bf16),
        pltpu.VMEM((units, 3, frames, LANES), bf16),
        pltpu.VMEM((n, 3, frames, LANES), bf16),
        pltpu.VMEM((n, frames, LANES), bf16),
        pltpu.VMEM((nx, units, frames, LANES), bf16),
        pltpu.VMEM((slabs, rows, cols), bf16),
        pltpu.VMEM((slabs, rows, cols), bf16),
        pltpu.VMEM((rows, width), f32),
        pltpu.VMEM((recs, frames, chans), bf16),
        pltpu.VMEM((recs, frames + 2 * RIM, chans), f32),
        pltpu.VMEM((2, recs, RIM, chans), bf16),
        pltpu.VMEM((recs, frames, chans), bf16),
        pltpu.VMEM((slabs, recs, nx, 2, rm, cols), bf16),
        pltpu.VMEM((slabs, recs, nx, rm, cols), bf16),
        pltpu.VMEM((slabs, nx, recs, rm, cols), bf16),
        pltpu.VMEM((slabs, nx, recs, rm, cols), bf16),
        dma((6,)),
        dma((3, n)), dma((3, n)),
        dma((nx,)), dma((nx,)),
        dma((n,)), dma((n,)),
        dma((nx, n)), dma((nx, n)),
        dma((slabs,)), dma((slabs,)),
        dma((2,)), dma((2,)),
        dma((slabs,)), dma((slabs,)),
        dma((slabs, nx)), dma((slabs, nx)),
    ]
    return pl.pallas_call(
        functools.partial(fused, n, nx, recs, frames, taps, cols),
        out_shape=jax.ShapeDtypeStruct((recs, rm, width), bf16),
        in_specs=[
            vmem, pl.BlockSpec(memory_space=pltpu.SMEM), vmem, hbm, hbm, vmem, hbm, vmem, vmem, vmem, hbm, vmem,
        ],
        out_specs=vmem,
        scratch_shapes=scratch,
        compiler_params=pltpu.CompilerParams(
            collective_id=0, has_side_effects=True, vmem_limit_bytes=56 * 2**20
        ),
    )(
        features.reshape(rows, width), frame_counts, attn_gain, w_qkv, w_out, conv_gain, w_glu, kernel,
        bn_scale, bn_shift, w_pw, clip_level,
    )


def solution(mesh):
    return jax.shard_map(
        functools.partial(shards, mesh.shape["ctx"], mesh.shape["mp"]),
        mesh=mesh,
        in_specs=(
            P("groups", "ctx", None),
            P("groups"),
            P(),
            P(None, None, "mp"),
            P("mp", None),
            P(),
            P(None, None, "mp"),
            P(None, "mp"),
            P("mp"),
            P("mp"),
            P("mp", None),
            P(),
        ),
        out_specs=P("groups", ("ctx", "mp"), None),
        check_vma=False,
    )
```

```python
import functools

import jax
import jax.numpy as jnp
from jax import lax
from jax.experimental import pallas as pl
from jax.experimental.pallas import tpu as pltpu
from jax.sharding import PartitionSpec as P

MESH = pl.DeviceIdType.MESH
HEAD_DIM = 64
LANES = 128
RIM = 16
W_CHUNKS = 2
epsilon = 1e-05
masked_score = -1e30
f32 = jnp.float32
bf16 = jnp.bfloat16


def loop(count, step):
    if count <= 2:
        for i in range(count):
            step(i)
    else:
        lax.fori_loop(0, count, lambda i, carry: (step(i), carry)[1], 0)


def when(cond):
    if cond is True:
        return lambda f: f()
    return lambda f: pl.when(cond)(lambda: f())


def normalise(values, gain):
    centred = values - jnp.mean(values, axis=-1, keepdims=True)
    variance = jnp.mean(centred * centred, axis=-1, keepdims=True)
    return (centred * lax.rsqrt(variance + epsilon) * gain).astype(bf16)


def fused(
    n, nx, ng, recs, frames, taps,
    feat_h, counts_h, ag_h, wqkv_h, wout_h, cg_h, wglu_h, ker_h, bns_h, bnb_h, wpw_h, clip_h, out,
    feat, counts, ag, cg, ker, bns, bnb, clip,
    wqkv, wo, wglu, wpw, xn, qkv_s, qkv_r, atto, att_all, w_s, tot_s, parts, sibs, res, gb, gp, halo, act,
    p5, s5, sum5, x5,
    ld, sm, qs, qr, wos, wor, ys, yr, zs, zr, fs, fr, ss, sr, hs, hr, bs, br, es, er,
):
    c = lax.axis_index("ctx")
    m = lax.axis_index("mp")
    x = lax.div(m, 2)
    core = lax.rem(m, 2)
    g_rank = lax.axis_index("groups")
    sibling = {"mp": x * 2 + (1 - core)}
    rows, width = feat.shape
    pairs = wqkv.shape[2] // LANES
    units = recs * pairs
    chans = gb.shape[2]
    rm = frames // (2 * nx)
    group = min(recs, 2)
    block = group * frames

    def ctx_at(k):
        return lax.rem(c + k, n)

    def has_unit(rank):
        return True if units == n else rank < units

    def x_peer(k):
        return {"mp": lax.rem(x + k, nx) * 2 + core}

    def y_peer(k):
        return {"groups": lax.rem(g_rank + k, ng)}

    def remote(src, dst, send, recv, where):
        return pltpu.make_async_remote_copy(
            src_ref=src, dst_ref=dst, send_sem=send, recv_sem=recv, device_id=where, device_id_type=MESH
        )

    barrier = pltpu.get_barrier_semaphore()
    for k in range(1, n):
        pl.semaphore_signal(barrier, inc=1, device_id={"ctx": ctx_at(k)}, device_id_type=MESH)
    for k in range(1, nx):
        pl.semaphore_signal(barrier, inc=1, device_id=x_peer(k), device_id_type=MESH)
    for k in range(1, ng):
        pl.semaphore_signal(barrier, inc=1, device_id=y_peer(k), device_id_type=MESH)
    pl.semaphore_signal(barrier, inc=1, device_id=sibling, device_id_type=MESH)

    pairs_in = [(feat_h, feat), (ag_h, ag), (counts_h, counts), (cg_h, cg), (ker_h, ker), (bns_h, bns),
                (bnb_h, bnb), (clip_h, clip)]
    smalls = [pltpu.make_async_copy(src, dst, sm.at[i]) for i, (src, dst) in enumerate(pairs_in)]
    loads = [pltpu.make_async_copy(wqkv_h.at[i], wqkv.at[i], ld.at[i]) for i in range(3)]
    loads.append(pltpu.make_async_copy(wglu_h, wglu, ld.at[3]))
    loads.append(pltpu.make_async_copy(wpw_h, wpw, ld.at[4]))
    loads.append(pltpu.make_async_copy(wout_h, wo.at[x], ld.at[5]))
    smalls[0].start()
    smalls[1].start()
    for i in (1, 0, 2):
        loads[i].start()
    for copy in smalls[2:]:
        copy.start()
    for i in (5, 3, 4):
        loads[i].start()
    smalls[0].wait()
    smalls[1].wait()

    gain = ag[...].reshape(1, width)

    def norm_in(i):
        at = pl.ds(pl.multiple_of(i * 32, 32), 32)
        xn[at, :] = normalise(feat[at, :].astype(f32), gain)

    lax.fori_loop(0, rows // 32, lambda i, carry: (norm_in(i), carry)[1], 0, unroll=4)

    pl.semaphore_wait(barrier, n - 1 + nx - 1 + ng - 1 + 1)

    local = wo.shape[1]
    share = local // ng
    sub = share // W_CHUNKS

    def w_rows(rank, chunk):
        return pl.ds(pl.multiple_of(rank * share + chunk * sub, sub), sub)

    w_copies = {}
    for chunk in range(W_CHUNKS):
        for k in range(1, nx):
            at = w_rows(g_rank, chunk)
            copy = remote(wout_h.at[at, :], wo.at[x, at, :], wos.at[k, chunk], wor.at[k, chunk], x_peer(k))
            copy.start()
            w_copies[k, chunk] = copy
    y_copies = []

    def hand_on(chunk):
        for k in range(1, nx):
            w_copies[k, chunk].wait_recv()
            at = w_rows(g_rank, chunk)
            held = wo.at[lax.rem(x - k + nx, nx), at, :]
            for j in range(1, ng):
                copy = remote(held, held, ys.at[k, chunk, j], yr.at[k, chunk, j], y_peer(j))
                copy.start()
                y_copies.append(copy)

    q_copies = []
    for i in (1, 0, 2):
        loads[i].wait()

        def project(g, i=i):
            at = pl.ds(pl.multiple_of(g * block, block), block)
            made = jnp.dot(xn[at, :], wqkv[i], preferred_element_type=f32).astype(bf16)
            for r in range(group):
                for p in range(pairs):
                    piece = made[r * frames : (r + 1) * frames, p * LANES : (p + 1) * LANES]
                    qkv_s[(g * group + r) * pairs + p, i] = piece

        loop(recs // group, project)
        for k in range(1, n):
            dest = ctx_at(k)
            copy = remote(
                qkv_s.at[lax.rem(dest, units), i], qkv_r.at[c, i], qs.at[i, k], qr.at[i, k], {"ctx": dest}
            )
            when(has_unit(dest))(copy.start)
            q_copies.append((copy, dest, i))

        @when(has_unit(c))
        def _(i=i):
            qkv_r[c, i] = qkv_s[lax.rem(c, units), i]

    z_copies = [
        remote(atto.at[k], att_all.at[x, lax.rem(c, units)], zs.at[k], zr.at[k], {"ctx": ctx_at(k)})
        for k in range(1, n)
    ]

    hand_on(0)
    smalls[2].wait()

    def arrived(which):
        @when(has_unit(c))
        def _():
            for copy, _dest, i in q_copies:
                if i in which:
                    copy.wait_recv()

    arrived((1, 0))
    own_rec = lax.div(lax.rem(c, units), pairs)
    live_keys = counts[own_rec]
    key_count = n * frames
    lane = lax.broadcasted_iota(jnp.int32, (1, LANES), 1)
    low = lane < HEAD_DIM
    seen = lax.broadcasted_iota(jnp.int32, (1, key_count), 1) < live_keys
    slots = w_s.shape[0]

    def weigh(k0, slot):
        keys = qkv_r[:, 1].reshape(key_count, LANES)
        queries = jnp.concatenate([qkv_r[ctx_at(k0), 0], qkv_r[ctx_at(k0 + 1), 0]], axis=0)
        for h in range(2):
            mine = jnp.where(low if h == 0 else jnp.logical_not(low), queries, jnp.zeros((), bf16))
            scores = lax.dot_general(mine, keys, (((1,), (1,)), ((), ())), preferred_element_type=f32)
            scores = jnp.where(seen, scores, masked_score)
            top = jnp.max(scores, axis=-1, keepdims=True)
            weights = jnp.exp((scores - top) * (HEAD_DIM**-0.5))
            tot_s[slot, h] = jnp.sum(weights, axis=-1, keepdims=True)
            w_s[slot, h] = weights.astype(bf16)

    def mix(k0, slot):
        values = qkv_r[:, 2].reshape(key_count, LANES)
        heads = [
            jnp.dot(w_s[slot, h], values, preferred_element_type=f32) / tot_s[slot, h] for h in range(2)
        ]
        both = jnp.where(low, heads[0], heads[1]).astype(bf16)
        atto[k0] = both[:frames]
        atto[k0 + 1] = both[frames:]

    def give(k):
        if k == 0:
            att_all[x, lax.rem(c, units)] = atto[0]
        else:
            z_copies[k - 1].start()

    starts = list(range(0, n, 2))
    if slots > 1:
        @when(has_unit(c))
        def _():
            for slot, k0 in enumerate(starts):
                weigh(k0, slot)

    for chunk in range(1, W_CHUNKS):
        hand_on(chunk)
    arrived((2,))

    @when(has_unit(c))
    def _():
        if slots > 1:
            for slot, k0 in reversed(list(enumerate(starts))):
                mix(k0, slot)
                give(k0 + 1)
                give(k0)
        else:
            def whole_step(i, carry):
                weigh(2 * i, 0)
                mix(2 * i, 0)
                return carry

            lax.fori_loop(0, n // 2, whole_step, 0)
            for k in range(n):
                give(k)

    f_copies = []
    for k in range(n):
        unit = lax.rem(c - k + n, n)
        spot = lax.rem(unit, units)

        @when(has_unit(unit))
        def _(k=k, unit=unit, spot=spot):
            if k > 0:
                remote(atto.at[k], att_all.at[x, spot], zs.at[k], zr.at[k], {"ctx": unit}).wait_recv()
            for j in range(1, nx):
                remote(
                    att_all.at[x, spot], att_all.at[x, spot], fs.at[j, k], fr.at[j, k], x_peer(j)
                ).start()

        for j in range(1, nx):
            f_copies.append(
                (remote(att_all.at[x, spot], att_all.at[x, spot], fs.at[j, k], fr.at[j, k], x_peer(j)), unit)
            )

    loads[5].wait()
    for copy in y_copies:
        copy.wait_recv()
    for copy, unit in f_copies:
        when(has_unit(unit))(copy.wait_recv)

    s_copies = []
    for rec in range(recs):
        gathered = jnp.concatenate(
            [att_all[i, rec * pairs + p] for i in range(nx) for p in range(pairs)], axis=1
        )
        parts[rec] = jnp.dot(
            gathered, wo[...].reshape(nx * pairs * LANES, width), preferred_element_type=f32
        ).astype(bf16)
        copy = remote(parts.at[rec], sibs.at[rec], ss.at[rec], sr.at[rec], sibling)
        copy.start()
        s_copies.append(copy)

    smalls[3].wait()
    conv_gain = cg[...].reshape(1, width)
    for rec in range(recs):
        s_copies[rec].wait_recv()

        def norm_conv(i, rec=rec):
            near = pl.ds(pl.multiple_of(i * 32, 32), 32)
            at = pl.ds(pl.multiple_of(rec * frames + i * 32, 32), 32)
            total = feat[at, :].astype(f32) + (parts[rec, near, :].astype(f32) + sibs[rec, near, :].astype(f32))
            res[at, :] = total
            xn[at, :] = normalise(total, conv_gain)

        lax.fori_loop(0, frames // 32, lambda i, carry: (norm_conv(i), carry)[1], 0, unroll=4)

    loads[3].wait()
    first_frame = c * frames
    frame_ids = first_frame + lax.broadcasted_iota(jnp.int32, (frames, 1), 0)

    def gate(g):
        at = pl.ds(pl.multiple_of(g * block, block), block)
        value_half = jnp.dot(xn[at, :], wglu[0], preferred_element_type=f32)
        gate_half = jnp.dot(xn[at, :], wglu[1], preferred_element_type=f32)
        gated = value_half * jax.nn.sigmoid(gate_half)
        for r in range(group):
            rec = g * group + r
            kept = jnp.where(frame_ids < counts[rec], gated[r * frames : (r + 1) * frames], 0.0).astype(bf16)
            gb[rec] = kept
            gp[rec, RIM : RIM + frames, :] = kept.astype(f32)

    loop(recs // group, gate)

    def up():
        return remote(gb.at[:, frames - RIM : frames, :], halo.at[0], hs.at[0], hr.at[0], {"ctx": lax.rem(c + 1, n)})

    def down():
        return remote(gb.at[:, 0:RIM, :], halo.at[1], hs.at[1], hr.at[1], {"ctx": lax.rem(c + n - 1, n)})

    @pl.when(c < n - 1)
    def _():
        up().start()

    @pl.when(c > 0)
    def _():
        down().start()

    for copy in smalls[4:]:
        copy.wait()
    scale = bns[...].reshape(1, chans)
    shift = bnb[...].reshape(1, chans)

    def depthwise(rec, start, count):
        for lo in range(0, chans, LANES):
            hi = min(lo + LANES, chans)
            total = jnp.zeros((count, hi - lo), f32)
            for tap in range(taps):
                begin = start + tap + RIM - taps // 2
                total = total + gp[rec, begin : begin + count, lo:hi] * ker[tap : tap + 1, lo:hi]
            v = total * scale[:, lo:hi] + shift[:, lo:hi]
            act[rec, start : start + count, lo:hi] = (v * jax.nn.sigmoid(v)).astype(bf16)

    def rim():
        @pl.when(c > 0)
        def _():
            up().wait_recv()

        @pl.when(c == 0)
        def _():
            halo[0] = jnp.zeros(halo.shape[1:], bf16)

        @pl.when(c < n - 1)
        def _():
            down().wait_recv()

        @pl.when(c == n - 1)
        def _():
            halo[1] = jnp.zeros(halo.shape[1:], bf16)

    b_copies = []
    e_copies = []

    def pass_on(rec):
        b_copies[rec].wait_recv()
        for i in range(nx):
            sum5[rec, i] = (p5[rec, i, core].astype(f32) + s5[rec, i].astype(f32)).astype(bf16)
        for k in range(1, nx):
            copy = remote(sum5.at[rec, lax.rem(x + k, nx)], x5.at[rec, k], es.at[rec, k], er.at[rec, k], x_peer(k))
            copy.start()
            e_copies.append(copy)

    for rec in range(recs):
        depthwise(rec, RIM, frames - 2 * RIM)
        if rec == 0:
            rim()
            loads[4].wait()
        gp[rec, 0:RIM, :] = halo[0, rec].astype(f32)
        gp[rec, RIM + frames : 2 * RIM + frames, :] = halo[1, rec].astype(f32)
        depthwise(rec, 0, RIM)
        depthwise(rec, frames - RIM, RIM)
        if rec > 0:
            pass_on(rec - 1)
        made = jnp.dot(act[rec], wpw[...], preferred_element_type=f32)
        p5[rec] = made.reshape(nx, 2, rm, width).astype(bf16)
        copy = remote(p5.at[rec, :, 1 - core], s5.at[rec], bs.at[rec], br.at[rec], sibling)
        copy.start()
        b_copies.append(copy)
    pass_on(recs - 1)

    row_start = pl.multiple_of(m * rm, rm)
    mine_ids = first_frame + row_start + lax.broadcasted_iota(jnp.int32, (rm, 1), 0)
    bound = clip[...].reshape(1, width).astype(f32) / 16.0
    for rec in range(recs):
        for k in range(1, nx):
            e_copies[rec * (nx - 1) + k - 1].wait_recv()
        at = pl.ds(pl.multiple_of(rec * frames + row_start, rm), rm)
        total = res[at, :] + sum5[rec, x].astype(f32)
        for k in range(1, nx):
            total = total + x5[rec, k].astype(f32)
        clipped = jnp.minimum(jnp.maximum(total, -bound), bound)
        out[rec] = jnp.where(mine_ids < counts[rec], clipped, 0.0).astype(bf16)

    for copy, dest, _i in q_copies:
        when(has_unit(dest))(copy.wait_send)

    @when(has_unit(c))
    def _():
        for copy in z_copies:
            copy.wait_send()

    for copy, unit in f_copies:
        when(has_unit(unit))(copy.wait_send)
    for copy in list(w_copies.values()) + y_copies + s_copies + b_copies + e_copies:
        copy.wait_send()

    @pl.when(c < n - 1)
    def _():
        up().wait_send()

    @pl.when(c > 0)
    def _():
        down().wait_send()


def shards(n, mp, ng, features, frame_counts, attn_gain, w_qkv, w_out, conv_gain, w_glu, kernel, bn_scale, bn_shift, w_pw, clip_level):
    recs, frames, width = features.shape
    nx = mp // 2
    rows = recs * frames
    local = w_qkv.shape[2]
    units = recs * local // LANES
    chans = w_glu.shape[2]
    rm = frames // mp
    taps = kernel.shape[0]
    vmem = pl.BlockSpec(memory_space=pltpu.VMEM)
    hbm = pl.BlockSpec(memory_space=pl.ANY)
    dma = pltpu.SemaphoreType.DMA
    slots = n // 2 if n <= 4 else 1
    scratch = [
        pltpu.VMEM((rows, width), bf16),
        pltpu.SMEM(frame_counts.shape, jnp.int32),
        pltpu.VMEM(attn_gain.shape, f32),
        pltpu.VMEM(conv_gain.shape, f32),
        pltpu.VMEM(kernel.shape, f32),
        pltpu.VMEM(bn_scale.shape, f32),
        pltpu.VMEM(bn_shift.shape, f32),
        pltpu.VMEM(clip_level.shape, jnp.int32),
        pltpu.VMEM(w_qkv.shape, bf16),
        pltpu.VMEM((nx, local, width), bf16),
        pltpu.VMEM(w_glu.shape, bf16),
        pltpu.VMEM(w_pw.shape, bf16),
        pltpu.VMEM((rows, width), bf16),
        pltpu.VMEM((units, 3, frames, LANES), bf16),
        pltpu.VMEM((n, 3, frames, LANES), bf16),
        pltpu.VMEM((n, frames, LANES), bf16),
        pltpu.VMEM((nx, units, frames, LANES), bf16),
        pltpu.VMEM((slots, 2, 2 * frames, n * frames), bf16),
        pltpu.VMEM((slots, 2, 2 * frames, 1), f32),
        pltpu.VMEM((recs, frames, width), bf16),
        pltpu.VMEM((recs, frames, width), bf16),
        pltpu.VMEM((rows, width), f32),
        pltpu.VMEM((recs, frames, chans), bf16),
        pltpu.VMEM((recs, frames + 2 * RIM, chans), f32),
        pltpu.VMEM((2, recs, RIM, chans), bf16),
        pltpu.VMEM((recs, frames, chans), bf16),
        pltpu.VMEM((recs, nx, 2, rm, width), bf16),
        pltpu.VMEM((recs, nx, rm, width), bf16),
        pltpu.VMEM((recs, nx, rm, width), bf16),
        pltpu.VMEM((recs, nx, rm, width), bf16),
        dma((6,)),
        dma((8,)),
        dma((3, n)), dma((3, n)),
        dma((nx, W_CHUNKS)), dma((nx, W_CHUNKS)),
        dma((nx, W_CHUNKS, ng)), dma((nx, W_CHUNKS, ng)),
        dma((n,)), dma((n,)),
        dma((nx, n)), dma((nx, n)),
        dma((recs,)), dma((recs,)),
        dma((2,)), dma((2,)),
        dma((recs,)), dma((recs,)),
        dma((recs, nx)), dma((recs, nx)),
    ]
    return pl.pallas_call(
        functools.partial(fused, n, nx, ng, recs, frames, taps),
        out_shape=jax.ShapeDtypeStruct((recs, rm, width), bf16),
        in_specs=[hbm] * 12,
        out_specs=vmem,
        scratch_shapes=scratch,
        compiler_params=pltpu.CompilerParams(
            collective_id=0, has_side_effects=True, vmem_limit_bytes=56 * 2**20
        ),
    )(
        features.reshape(rows, width), frame_counts, attn_gain, w_qkv, w_out, conv_gain, w_glu, kernel,
        bn_scale, bn_shift, w_pw, clip_level,
    )


def solution(mesh):
    return jax.shard_map(
        functools.partial(shards, mesh.shape["ctx"], mesh.shape["mp"], mesh.shape["groups"]),
        mesh=mesh,
        in_specs=(
            P("groups", "ctx", None),
            P("groups"),
            P(),
            P(None, None, "mp"),
            P("mp", None),
            P(),
            P(None, None, "mp"),
            P(None, "mp"),
            P("mp"),
            P("mp"),
            P("mp", None),
            P(),
        ),
        out_specs=P("groups", ("ctx", "mp"), None),
        check_vma=False,
    )
```

```python
import functools

import jax
import jax.numpy as jnp
from jax import lax
from jax.experimental import pallas as pl
from jax.experimental.pallas import tpu as pltpu
from jax.sharding import PartitionSpec as P

MESH = pl.DeviceIdType.MESH
HEAD_DIM = 64
LANES = 128
RIM = 16
W_CHUNKS = 4
epsilon = 1e-05
masked_score = -1e30
f32 = jnp.float32
bf16 = jnp.bfloat16


def swap_halves(values):
    return pltpu.roll(values, HEAD_DIM, axis=1)


def normalise(values, gain):
    centred = values - jnp.mean(values, axis=-1, keepdims=True)
    variance = jnp.mean(centred * centred, axis=-1, keepdims=True)
    return (centred * lax.rsqrt(variance + epsilon) * gain).astype(bf16)


def fused(
    n, nx, ng, recs, frames, taps,
    feat_h, counts_h, ag_h, wqkv_h, wout_h, cg_h, wglu_h, ker_h, bns_h, bnb_h, wpw_h, clip_h, out,
    feat, counts, ag, cg, ker, bns, bnb, clip,
    wqkv, wo, wglu, wpw, xn, qk_s, v_s, qk_r, v_r, atto, att_all, w_s, tot_s, parts, sibs, res, gb, gp, halo, act,
    p5, s5, sum5, x5,
    ld, sm, qs, qr, vs, vr, wos, wor, ys, yr, zs, zr, fs, fr, ss, sr, hs, hr, bs, br, es, er,
):
    c = lax.axis_index("ctx")
    m = lax.axis_index("mp")
    x = lax.div(m, 2)
    core = lax.rem(m, 2)
    g_rank = lax.axis_index("groups")
    sibling = {"mp": x * 2 + (1 - core)}
    rows, width = feat.shape
    heads = wqkv.shape[2] // HEAD_DIM
    pairs = heads // 2
    phases = recs * heads // n
    per_phase = recs // phases
    chans = gb.shape[2]
    rm = frames // (2 * nx)
    half = frames // 2

    def ctx_at(k):
        return lax.rem(c + k, n)

    def x_peer(k):
        return {"mp": lax.rem(x + k, nx) * 2 + core}

    def y_peer(k):
        return {"groups": lax.rem(g_rank + k, ng)}

    def remote(src, dst, send, recv, where):
        return pltpu.make_async_remote_copy(
            src_ref=src, dst_ref=dst, send_sem=send, recv_sem=recv, device_id=where, device_id_type=MESH
        )

    barrier = pltpu.get_barrier_semaphore()
    for k in range(1, n):
        pl.semaphore_signal(barrier, inc=1, device_id={"ctx": ctx_at(k)}, device_id_type=MESH)
    for k in range(1, nx):
        pl.semaphore_signal(barrier, inc=1, device_id=x_peer(k), device_id_type=MESH)
    for k in range(1, ng):
        pl.semaphore_signal(barrier, inc=1, device_id=y_peer(k), device_id_type=MESH)
    pl.semaphore_signal(barrier, inc=1, device_id=sibling, device_id_type=MESH)

    pairs_in = [(feat_h, feat), (ag_h, ag), (counts_h, counts), (cg_h, cg), (ker_h, ker), (bns_h, bns),
                (bnb_h, bnb), (clip_h, clip)]
    smalls = [pltpu.make_async_copy(src, dst, sm.at[i]) for i, (src, dst) in enumerate(pairs_in)]
    loads = [pltpu.make_async_copy(wqkv_h.at[i], wqkv.at[i], ld.at[i]) for i in range(3)]
    loads.append(pltpu.make_async_copy(wglu_h, wglu, ld.at[3]))
    loads.append(pltpu.make_async_copy(wpw_h, wpw, ld.at[4]))
    loads.append(pltpu.make_async_copy(wout_h, wo.at[x], ld.at[5]))
    smalls[0].start()
    smalls[1].start()
    for i in (1, 0, 2):
        loads[i].start()
    for copy in smalls[2:]:
        copy.start()
    for i in (5, 3, 4):
        loads[i].start()
    smalls[0].wait()
    smalls[1].wait()

    gain = ag[...].reshape(1, width)

    lane = lax.broadcasted_iota(jnp.int32, (1, LANES), 1)
    low = lane < HEAD_DIM

    def norm_in(f):
        def strip(i, carry):
            at = pl.ds(pl.multiple_of(f * per_phase * frames + i * 32, 32), 32)
            xn[at, :] = normalise(feat[at, :].astype(f32), gain)
            return carry

        lax.fori_loop(0, per_phase * frames // 32, strip, 0, unroll=4)

    norm_in(0)
    pl.semaphore_wait(barrier, n - 1 + nx - 1 + ng - 1 + 1)

    local = wo.shape[1]
    share = local // ng
    sub = share // W_CHUNKS

    def w_rows(rank, chunk):
        return pl.ds(pl.multiple_of(rank * share + chunk * sub, sub), sub)

    w_copies = {}
    for chunk in range(W_CHUNKS):
        for k in range(1, nx):
            at = w_rows(g_rank, chunk)
            copy = remote(wout_h.at[at, :], wo.at[x, at, :], wos.at[k, chunk], wor.at[k, chunk], x_peer(k))
            copy.start()
            w_copies[k, chunk] = copy
    y_copies = []

    def hand_on(chunk):
        for k in range(1, nx):
            w_copies[k, chunk].wait_recv()
            at = w_rows(g_rank, chunk)
            held = wo.at[lax.rem(x - k + nx, nx), at, :]
            for j in range(1, ng):
                copy = remote(held, held, ys.at[k, chunk, j], yr.at[k, chunk, j], y_peer(j))
                copy.start()
                y_copies.append(copy)

    def rows_of(rec):
        return pl.ds(rec * frames, frames)

    def columns(values, p):
        return values[:, p * LANES : (p + 1) * LANES]

    def send_units(f, src, dst, send, recv):
        copies = []
        for k in range(1, n):
            dest = ctx_at(k)
            copy = remote(src.at[f * n + dest], dst.at[f, c], send.at[f, k], recv.at[f, k], {"ctx": dest})
            copy.start()
            copies.append(copy)
        dst[f, c] = src[f * n + c]
        return copies

    qk_copies = []
    v_copies = []
    for f in range(phases):
        if f > 0:
            norm_in(f)
        if f == 0:
            loads[1].wait()
            loads[0].wait()
        mine = range(f * per_phase, (f + 1) * per_phase)
        for rec in mine:
            keys = jnp.dot(xn[rows_of(rec), :], wqkv[1], preferred_element_type=f32)
            queries = jnp.dot(xn[rows_of(rec), :], wqkv[0], preferred_element_type=f32)
            for p in range(pairs):
                q, k = columns(queries, p), columns(keys, p)
                qk_s[rec * heads + 2 * p] = jnp.where(low, q, swap_halves(k)).astype(bf16)
                qk_s[rec * heads + 2 * p + 1] = jnp.where(low, swap_halves(q), k).astype(bf16)
        qk_copies.append(send_units(f, qk_s, qk_r, qs, qr))
        if f == 0:
            loads[2].wait()
        for rec in mine:
            made = jnp.dot(xn[rows_of(rec), :], wqkv[2], preferred_element_type=f32)
            for p in range(pairs):
                v = columns(made, p)
                v_s[rec * heads + 2 * p] = jnp.where(low, v[:half], swap_halves(v[half:])).astype(bf16)
                v_s[rec * heads + 2 * p + 1] = jnp.where(low, swap_halves(v[:half]), v[half:]).astype(bf16)
        v_copies.append(send_units(f, v_s, v_r, vs, vr))

    key_count = n * frames
    slots = w_s.shape[0]
    starts = list(range(0, n, 2))

    def weigh(f, k0, slot):
        both = qk_r[f].reshape(key_count, LANES)
        keys = swap_halves(both.astype(f32)).astype(bf16)
        queries = jnp.concatenate([qk_r[f, ctx_at(k0)], qk_r[f, ctx_at(k0 + 1)]], axis=0)
        queries = jnp.where(low, queries, jnp.zeros((), bf16))
        scores = lax.dot_general(queries, keys, (((1,), (1,)), ((), ())), preferred_element_type=f32)
        live_keys = counts[lax.div(f * n + c, heads)]
        seen = lax.broadcasted_iota(jnp.int32, (1, key_count), 1) < live_keys
        scores = jnp.where(seen, scores, masked_score)
        top = jnp.max(scores, axis=-1, keepdims=True)
        weights = jnp.exp((scores - top) * (HEAD_DIM**-0.5))
        tot_s[slot] = jnp.sum(weights, axis=-1, keepdims=True)
        w_s[slot] = weights.astype(bf16)

    def mix(f, k0, slot):
        folded = v_r[f].astype(f32)
        late = swap_halves(folded.reshape(n * half, LANES)).reshape(n, half, LANES)
        values = jnp.concatenate([folded, late], axis=1).reshape(key_count, LANES).astype(bf16)
        mixed = jnp.dot(w_s[slot], values, preferred_element_type=f32) / tot_s[slot]
        for i in range(2):
            piece = mixed[i * frames : (i + 1) * frames]
            atto[f, k0 + i] = jnp.where(low, piece[:half], swap_halves(piece[half:])).astype(bf16)

    z_copies = [
        [
            remote(atto.at[f, k], att_all.at[x, f * n + c], zs.at[f, k], zr.at[f, k], {"ctx": ctx_at(k)})
            for k in range(1, n)
        ]
        for f in range(phases)
    ]

    def give(f, k):
        if k == 0:
            att_all[x, f * n + c] = atto[f, 0]
        else:
            z_copies[f][k - 1].start()

    f_copies = [[] for f in range(phases)]

    def forward(f):
        for k in range(n):
            spot = f * n + lax.rem(c - k + n, n)
            if k > 0:
                z_copies[f][k - 1].wait_recv()
            for j in range(1, nx):
                held = att_all.at[x, spot]
                copy = remote(held, held, fs.at[j, f, k], fr.at[j, f, k], x_peer(j))
                copy.start()
                f_copies[f].append(copy)

    chunks = list(range(W_CHUNKS))
    hand_on(chunks.pop(0))
    hand_on(chunks.pop(0))
    smalls[2].wait()
    for f in range(phases):
        for copy in qk_copies[f]:
            copy.wait_recv()
        if slots > 1:
            for slot, k0 in enumerate(starts):
                weigh(f, k0, slot)
        if f > 0:
            forward(f - 1)
        elif chunks:
            hand_on(chunks.pop(0))
        for copy in v_copies[f]:
            copy.wait_recv()
        if slots > 1:
            for slot, k0 in enumerate(starts):
                mix(f, k0, slot)
                give(f, k0 + 1)
                give(f, k0)
        else:
            def whole_step(i, carry, f=f):
                weigh(f, 2 * i, 0)
                mix(f, 2 * i, 0)
                return carry

            lax.fori_loop(0, n // 2, whole_step, 0)
            for k in range(n):
                give(f, k)
        while chunks:
            hand_on(chunks.pop(0))

    for copy in smalls[3:]:
        copy.wait()
    conv_gain = cg[...].reshape(1, width)

    def unfold(i, unit, odd):
        piece = att_all[i, unit].astype(f32)
        turned = swap_halves(piece)
        return jnp.concatenate([turned, piece] if odd else [piece, turned], axis=0)

    s_copies = {}

    def project_out(rec):
        gathered = jnp.concatenate(
            [
                jnp.where(
                    low, unfold(i, rec * heads + 2 * p, False), unfold(i, rec * heads + 2 * p + 1, True)
                ).astype(bf16)
                for i in range(nx)
                for p in range(pairs)
            ],
            axis=1,
        )
        parts[rec] = jnp.dot(
            gathered, wo[...].reshape(nx * pairs * LANES, width), preferred_element_type=f32
        ).astype(bf16)
        s_copies[rec] = remote(parts.at[rec], sibs.at[rec], ss.at[rec], sr.at[rec], sibling)
        s_copies[rec].start()

    first_frame = c * frames
    frame_ids = first_frame + lax.broadcasted_iota(jnp.int32, (frames, 1), 0)

    def up(rec):
        return remote(
            gb.at[rec, frames - RIM : frames, :], halo.at[0, rec], hs.at[0, rec], hr.at[0, rec],
            {"ctx": lax.rem(c + 1, n)},
        )

    def down(rec):
        return remote(
            gb.at[rec, 0:RIM, :], halo.at[1, rec], hs.at[1, rec], hr.at[1, rec], {"ctx": lax.rem(c + n - 1, n)}
        )


    def gate(rec):
        s_copies[rec].wait_recv()

        def strip(i, carry):
            near = pl.ds(pl.multiple_of(i * 32, 32), 32)
            at = pl.ds(pl.multiple_of(rec * frames + i * 32, 32), 32)
            total = feat[at, :].astype(f32) + (parts[rec, near, :].astype(f32) + sibs[rec, near, :].astype(f32))
            res[at, :] = total
            xn[at, :] = normalise(total, conv_gain)
            return carry

        lax.fori_loop(0, frames // 32, strip, 0, unroll=4)
        value_half = jnp.dot(xn[rows_of(rec), :], wglu[0], preferred_element_type=f32)
        gate_half = jnp.dot(xn[rows_of(rec), :], wglu[1], preferred_element_type=f32)
        gated = value_half * jax.nn.sigmoid(gate_half)
        kept = jnp.where(frame_ids < counts[rec], gated, 0.0).astype(bf16)
        gb[rec] = kept
        gp[rec, RIM : RIM + frames, :] = kept.astype(f32)

        @pl.when(c < n - 1)
        def _():
            up(rec).start()

        @pl.when(c > 0)
        def _():
            down(rec).start()

    scale = bns[...].reshape(1, chans)
    shift = bnb[...].reshape(1, chans)

    def depthwise(rec, start, count):
        for lo in range(0, chans, LANES):
            hi = min(lo + LANES, chans)
            total = jnp.zeros((count, hi - lo), f32)
            for tap in range(taps):
                begin = start + tap + RIM - taps // 2
                total = total + gp[rec, begin : begin + count, lo:hi] * ker[tap : tap + 1, lo:hi]
            v = total * scale[:, lo:hi] + shift[:, lo:hi]
            act[rec, start : start + count, lo:hi] = (v * jax.nn.sigmoid(v)).astype(bf16)

    def rim(rec):
        @pl.when(c > 0)
        def _():
            up(rec).wait_recv()

        @pl.when(c == 0)
        def _():
            halo[0, rec] = jnp.zeros(halo.shape[2:], bf16)

        @pl.when(c < n - 1)
        def _():
            down(rec).wait_recv()

        @pl.when(c == n - 1)
        def _():
            halo[1, rec] = jnp.zeros(halo.shape[2:], bf16)

        gp[rec, 0:RIM, :] = halo[0, rec].astype(f32)
        gp[rec, RIM + frames : 2 * RIM + frames, :] = halo[1, rec].astype(f32)
        depthwise(rec, 0, RIM)
        depthwise(rec, frames - RIM, RIM)

    b_copies = []
    e_copies = []

    def pass_on(rec):
        b_copies[rec].wait_recv()
        for i in range(nx):
            sum5[rec, i] = (p5[rec, i, core].astype(f32) + s5[rec, i].astype(f32)).astype(bf16)
        for k in range(1, nx):
            copy = remote(sum5.at[rec, lax.rem(x + k, nx)], x5.at[rec, k], es.at[rec, k], er.at[rec, k], x_peer(k))
            copy.start()
            e_copies.append(copy)

    def interior(rec):
        depthwise(rec, RIM, frames - 2 * RIM)

    loads[5].wait()
    loads[3].wait()
    for copy in y_copies:
        copy.wait_recv()
    early = list(range((phases - 1) * per_phase))
    late = list(range((phases - 1) * per_phase, recs))
    for f in range(phases - 1):
        for copy in f_copies[f]:
            copy.wait_recv()
    for rec in early:
        project_out(rec)
    forward(phases - 1)
    for rec in early:
        gate(rec)
    for copy in f_copies[phases - 1]:
        copy.wait_recv()
    for rec in late:
        project_out(rec)
    for rec in early:
        interior(rec)
    for rec in late:
        gate(rec)
    loads[4].wait()
    for rec in range(recs):
        if rec in late:
            interior(rec)
        rim(rec)
        if rec > 0:
            pass_on(rec - 1)
        made = jnp.dot(act[rec], wpw[...], preferred_element_type=f32)
        p5[rec] = made.reshape(nx, 2, rm, width).astype(bf16)
        copy = remote(p5.at[rec, :, 1 - core], s5.at[rec], bs.at[rec], br.at[rec], sibling)
        copy.start()
        b_copies.append(copy)
    pass_on(recs - 1)

    row_start = pl.multiple_of(m * rm, rm)
    mine_ids = first_frame + row_start + lax.broadcasted_iota(jnp.int32, (rm, 1), 0)
    bound = clip[...].reshape(1, width).astype(f32) / 16.0
    for rec in range(recs):
        for k in range(1, nx):
            e_copies[rec * (nx - 1) + k - 1].wait_recv()
        at = pl.ds(pl.multiple_of(rec * frames + row_start, rm), rm)
        total = res[at, :] + sum5[rec, x].astype(f32)
        for k in range(1, nx):
            total = total + x5[rec, k].astype(f32)
        clipped = jnp.minimum(jnp.maximum(total, -bound), bound)
        out[rec] = jnp.where(mine_ids < counts[rec], clipped, 0.0).astype(bf16)

    waiting = list(w_copies.values()) + y_copies + list(s_copies.values()) + b_copies + e_copies
    for group in qk_copies + v_copies + z_copies + f_copies:
        waiting = waiting + group
    for copy in waiting:
        copy.wait_send()
    for rec in range(recs):
        @pl.when(c < n - 1)
        def _(rec=rec):
            up(rec).wait_send()

        @pl.when(c > 0)
        def _(rec=rec):
            down(rec).wait_send()


def shards(n, mp, ng, features, frame_counts, attn_gain, w_qkv, w_out, conv_gain, w_glu, kernel, bn_scale, bn_shift, w_pw, clip_level):
    recs, frames, width = features.shape
    nx = mp // 2
    rows = recs * frames
    local = w_qkv.shape[2]
    units = recs * local // HEAD_DIM
    phases = units // n
    half = frames // 2
    chans = w_glu.shape[2]
    rm = frames // mp
    taps = kernel.shape[0]
    vmem = pl.BlockSpec(memory_space=pltpu.VMEM)
    hbm = pl.BlockSpec(memory_space=pl.ANY)
    dma = pltpu.SemaphoreType.DMA
    slots = n // 2 if n <= 4 else 1
    scratch = [
        pltpu.VMEM((rows, width), bf16),
        pltpu.SMEM(frame_counts.shape, jnp.int32),
        pltpu.VMEM(attn_gain.shape, f32),
        pltpu.VMEM(conv_gain.shape, f32),
        pltpu.VMEM(kernel.shape, f32),
        pltpu.VMEM(bn_scale.shape, f32),
        pltpu.VMEM(bn_shift.shape, f32),
        pltpu.VMEM(clip_level.shape, jnp.int32),
        pltpu.VMEM(w_qkv.shape, bf16),
        pltpu.VMEM((nx, local, width), bf16),
        pltpu.VMEM(w_glu.shape, bf16),
        pltpu.VMEM(w_pw.shape, bf16),
        pltpu.VMEM((rows, width), bf16),
        pltpu.VMEM((units, frames, LANES), bf16),
        pltpu.VMEM((units, half, LANES), bf16),
        pltpu.VMEM((phases, n, frames, LANES), bf16),
        pltpu.VMEM((phases, n, half, LANES), bf16),
        pltpu.VMEM((phases, n, half, LANES), bf16),
        pltpu.VMEM((nx, units, half, LANES), bf16),
        pltpu.VMEM((slots, 2 * frames, n * frames), bf16),
        pltpu.VMEM((slots, 2 * frames, 1), f32),
        pltpu.VMEM((recs, frames, width), bf16),
        pltpu.VMEM((recs, frames, width), bf16),
        pltpu.VMEM((rows, width), f32),
        pltpu.VMEM((recs, frames, chans), bf16),
        pltpu.VMEM((recs, frames + 2 * RIM, chans), f32),
        pltpu.VMEM((2, recs, RIM, chans), bf16),
        pltpu.VMEM((recs, frames, chans), bf16),
        pltpu.VMEM((recs, nx, 2, rm, width), bf16),
        pltpu.VMEM((recs, nx, rm, width), bf16),
        pltpu.VMEM((recs, nx, rm, width), bf16),
        pltpu.VMEM((recs, nx, rm, width), bf16),
        dma((6,)),
        dma((8,)),
        dma((phases, n)), dma((phases, n)),
        dma((phases, n)), dma((phases, n)),
        dma((nx, W_CHUNKS)), dma((nx, W_CHUNKS)),
        dma((nx, W_CHUNKS, ng)), dma((nx, W_CHUNKS, ng)),
        dma((phases, n)), dma((phases, n)),
        dma((nx, phases, n)), dma((nx, phases, n)),
        dma((recs,)), dma((recs,)),
        dma((2, recs)), dma((2, recs)),
        dma((recs,)), dma((recs,)),
        dma((recs, nx)), dma((recs, nx)),
    ]
    return pl.pallas_call(
        functools.partial(fused, n, nx, ng, recs, frames, taps),
        out_shape=jax.ShapeDtypeStruct((recs, rm, width), bf16),
        in_specs=[hbm] * 12,
        out_specs=vmem,
        scratch_shapes=scratch,
        compiler_params=pltpu.CompilerParams(
            collective_id=0, has_side_effects=True, vmem_limit_bytes=56 * 2**20
        ),
    )(
        features.reshape(rows, width), frame_counts, attn_gain, w_qkv, w_out, conv_gain, w_glu, kernel,
        bn_scale, bn_shift, w_pw, clip_level,
    )


def solution(mesh):
    return jax.shard_map(
        functools.partial(shards, mesh.shape["ctx"], mesh.shape["mp"], mesh.shape["groups"]),
        mesh=mesh,
        in_specs=(
            P("groups", "ctx", None),
            P("groups"),
            P(),
            P(None, None, "mp"),
            P("mp", None),
            P(),
            P(None, None, "mp"),
            P(None, "mp"),
            P("mp"),
            P("mp"),
            P("mp", None),
            P(),
        ),
        out_specs=P("groups", ("ctx", "mp"), None),
        check_vma=False,
    )
```

```python
import functools

import jax
import jax.numpy as jnp
from jax import lax
from jax.experimental import pallas as pl
from jax.experimental.pallas import tpu as pltpu
from jax.sharding import PartitionSpec as P

MESH = pl.DeviceIdType.MESH
HEAD_DIM = 64
LANES = 128
RIM = 16
W_CHUNKS = 4
epsilon = 1e-05
masked_score = -1e30
f32 = jnp.float32
bf16 = jnp.bfloat16


def swap_halves(values):
    return pltpu.roll(values, HEAD_DIM, axis=1)


def normalise(values, gain):
    centred = values - jnp.mean(values, axis=-1, keepdims=True)
    variance = jnp.mean(centred * centred, axis=-1, keepdims=True)
    return (centred * lax.rsqrt(variance + epsilon) * gain).astype(bf16)


def fused(
    n, nx, ng, recs, frames, taps,
    feat_h, counts_h, ag_h, wqkv_h, wout_h, cg_h, wglu_h, ker_h, bns_h, bnb_h, wpw_h, clip_h, out,
    feat, counts, ag, cg, ker, bns, bnb, clip,
    wqkv, wo, wglu, wpw, xn, qk_s, v_s, qk_r, v_r, atto, att_all, w_s, tot_s, parts, sibs, res, gb, gp, halo, act,
    p5, s5, sum5, x5,
    ld, sm, qs, qr, vs, vr, wos, wor, ys, yr, zs, zr, fs, fr, ss, sr, hs, hr, bs, br, es, er,
):
    c = lax.axis_index("ctx")
    m = lax.axis_index("mp")
    x = lax.div(m, 2)
    core = lax.rem(m, 2)
    g_rank = lax.axis_index("groups")
    sibling = {"mp": x * 2 + (1 - core)}
    rows, width = feat.shape
    heads = wqkv.shape[2] // HEAD_DIM
    pairs = heads // 2
    phases = recs * heads // n
    per_phase = recs // phases
    chans = gb.shape[2]
    rm = frames // (2 * nx)
    half = frames // 2

    def ctx_at(k):
        return lax.rem(c + k, n)

    def x_peer(k):
        return {"mp": lax.rem(x + k, nx) * 2 + core}

    def y_peer(k):
        return {"groups": lax.rem(g_rank + k, ng)}

    def remote(src, dst, send, recv, where):
        return pltpu.make_async_remote_copy(
            src_ref=src, dst_ref=dst, send_sem=send, recv_sem=recv, device_id=where, device_id_type=MESH
        )

    barrier = pltpu.get_barrier_semaphore()
    for k in range(1, n):
        pl.semaphore_signal(barrier, inc=1, device_id={"ctx": ctx_at(k)}, device_id_type=MESH)
    for k in range(1, nx):
        pl.semaphore_signal(barrier, inc=1, device_id=x_peer(k), device_id_type=MESH)
    for k in range(1, ng):
        pl.semaphore_signal(barrier, inc=1, device_id=y_peer(k), device_id_type=MESH)
    pl.semaphore_signal(barrier, inc=1, device_id=sibling, device_id_type=MESH)

    pairs_in = [(feat_h, feat), (ag_h, ag), (counts_h, counts), (cg_h, cg), (ker_h, ker), (bns_h, bns),
                (bnb_h, bnb), (clip_h, clip)]
    smalls = [pltpu.make_async_copy(src, dst, sm.at[i]) for i, (src, dst) in enumerate(pairs_in)]
    loads = [pltpu.make_async_copy(wqkv_h.at[i], wqkv.at[i], ld.at[i]) for i in range(3)]
    loads.append(pltpu.make_async_copy(wglu_h, wglu, ld.at[3]))
    loads.append(pltpu.make_async_copy(wpw_h, wpw, ld.at[4]))
    loads.append(pltpu.make_async_copy(wout_h, wo.at[x], ld.at[5]))
    smalls[0].start()
    smalls[1].start()
    for i in (1, 0, 2):
        loads[i].start()
    for copy in smalls[2:]:
        copy.start()
    smalls[0].wait()
    smalls[1].wait()

    gain = ag[...].reshape(1, width)

    lane = lax.broadcasted_iota(jnp.int32, (1, LANES), 1)
    low = lane < HEAD_DIM

    def norm_in(i, carry):
        at = pl.ds(pl.multiple_of(i * 32, 32), 32)
        xn[at, :] = normalise(feat[at, :].astype(f32), gain)
        return carry

    lax.fori_loop(0, rows // 32, norm_in, 0, unroll=2)
    pl.semaphore_wait(barrier, n - 1 + nx - 1 + ng - 1 + 1)

    local = wo.shape[1]
    share = local // ng
    sub = share // W_CHUNKS

    def w_rows(rank, chunk):
        return pl.ds(pl.multiple_of(rank * share + chunk * sub, sub), sub)

    w_copies = {}
    for chunk in range(W_CHUNKS):
        for k in range(1, nx):
            at = w_rows(g_rank, chunk)
            copy = remote(wout_h.at[at, :], wo.at[x, at, :], wos.at[k, chunk], wor.at[k, chunk], x_peer(k))
            copy.start()
            w_copies[k, chunk] = copy
    y_copies = []

    def hand_on(chunk):
        for k in range(1, nx):
            w_copies[k, chunk].wait_recv()
            at = w_rows(g_rank, chunk)
            held = wo.at[lax.rem(x - k + nx, nx), at, :]
            for j in range(1, ng):
                copy = remote(held, held, ys.at[k, chunk, j], yr.at[k, chunk, j], y_peer(j))
                copy.start()
                y_copies.append(copy)

    def rows_of(rec):
        return pl.ds(pl.multiple_of(rec * frames, frames), frames)

    def columns(values, p):
        return values[:, p * LANES : (p + 1) * LANES]

    def unit_copies(f, src, dst, send, recv):
        return [
            remote(src.at[f * n + ctx_at(k)], dst.at[f, c], send.at[f, k], recv.at[f, k], {"ctx": ctx_at(k)})
            for k in range(1, n)
        ]

    for i in range(3):
        loads[i].wait()

    def make_units(f, carry):
        for r in range(per_phase):
            rec = f * per_phase + r
            keys = jnp.dot(xn[rows_of(rec), :], wqkv[1], preferred_element_type=f32)
            queries = jnp.dot(xn[rows_of(rec), :], wqkv[0], preferred_element_type=f32)
            for p in range(pairs):
                q, k = columns(queries, p), columns(keys, p)
                qk_s[rec * heads + 2 * p] = jnp.where(low, q, swap_halves(k)).astype(bf16)
                qk_s[rec * heads + 2 * p + 1] = jnp.where(low, swap_halves(q), k).astype(bf16)
        for copy in unit_copies(f, qk_s, qk_r, qs, qr):
            copy.start()
        qk_r[f, c] = qk_s[f * n + c]
        for r in range(per_phase):
            rec = f * per_phase + r
            made = jnp.dot(xn[rows_of(rec), :], wqkv[2], preferred_element_type=f32)
            for p in range(pairs):
                v = columns(made, p)
                v_s[rec * heads + 2 * p] = jnp.where(low, v[:half], swap_halves(v[half:])).astype(bf16)
                v_s[rec * heads + 2 * p + 1] = jnp.where(low, swap_halves(v[:half]), v[half:]).astype(bf16)
        for copy in unit_copies(f, v_s, v_r, vs, vr):
            copy.start()
        v_r[f, c] = v_s[f * n + c]
        return carry

    lax.fori_loop(0, phases, make_units, 0)
    qk_copies = [unit_copies(f, qk_s, qk_r, qs, qr) for f in range(phases)]
    v_copies = [unit_copies(f, v_s, v_r, vs, vr) for f in range(phases)]
    for i in (5, 3, 4):
        loads[i].start()

    key_count = n * frames
    slots = w_s.shape[0]
    starts = list(range(0, n, 2))

    def weigh(f, k0, slot):
        both = qk_r[f].reshape(key_count, LANES)
        keys = swap_halves(both.astype(f32)).astype(bf16)
        queries = jnp.concatenate([qk_r[f, ctx_at(k0)], qk_r[f, ctx_at(k0 + 1)]], axis=0)
        queries = jnp.where(low, queries, jnp.zeros((), bf16))
        scores = lax.dot_general(queries, keys, (((1,), (1,)), ((), ())), preferred_element_type=f32)
        live_keys = counts[lax.div(f * n + c, heads)]
        seen = lax.broadcasted_iota(jnp.int32, (1, key_count), 1) < live_keys
        scores = jnp.where(seen, scores, masked_score)
        top = jnp.max(scores, axis=-1, keepdims=True)
        weights = jnp.exp((scores - top) * (HEAD_DIM**-0.5))
        tot_s[slot] = jnp.sum(weights, axis=-1, keepdims=True)
        w_s[slot] = weights.astype(bf16)

    def mix(f, k0, slot):
        folded = v_r[f].astype(f32)
        late = swap_halves(folded.reshape(n * half, LANES)).reshape(n, half, LANES)
        values = jnp.concatenate([folded, late], axis=1).reshape(key_count, LANES).astype(bf16)
        mixed = jnp.dot(w_s[slot], values, preferred_element_type=f32) / tot_s[slot]
        for i in range(2):
            piece = mixed[i * frames : (i + 1) * frames]
            atto[f, k0 + i] = jnp.where(low, piece[:half], swap_halves(piece[half:])).astype(bf16)

    z_copies = [
        [
            remote(atto.at[f, k], att_all.at[x, f * n + c], zs.at[f, k], zr.at[f, k], {"ctx": ctx_at(k)})
            for k in range(1, n)
        ]
        for f in range(phases)
    ]

    def give(f, k):
        if k == 0:
            att_all[x, f * n + c] = atto[f, 0]
        else:
            z_copies[f][k - 1].start()

    f_copies = [[] for f in range(phases)]

    def forward(f):
        for k in range(n):
            spot = f * n + lax.rem(c - k + n, n)
            if k > 0:
                z_copies[f][k - 1].wait_recv()
            for j in range(1, nx):
                held = att_all.at[x, spot]
                copy = remote(held, held, fs.at[j, f, k], fr.at[j, f, k], x_peer(j))
                copy.start()
                f_copies[f].append(copy)

    chunks = list(range(W_CHUNKS))
    hand_on(chunks.pop(0))
    hand_on(chunks.pop(0))
    smalls[2].wait()
    for f in range(phases):
        for copy in qk_copies[f]:
            copy.wait_recv()
        if slots > 1:
            lax.fori_loop(0, slots, lambda i, carry, f=f: (weigh(f, 2 * i, i), carry)[1], 0)
        if f > 0:
            forward(f - 1)
        elif chunks:
            hand_on(chunks.pop(0))
        for copy in v_copies[f]:
            copy.wait_recv()
        if slots > 1:
            for slot, k0 in enumerate(starts):
                mix(f, k0, slot)
                give(f, k0 + 1)
                give(f, k0)
        else:
            def whole_step(i, carry, f=f):
                weigh(f, 2 * i, 0)
                mix(f, 2 * i, 0)
                return carry

            lax.fori_loop(0, n // 2, whole_step, 0)
            for k in range(n):
                give(f, k)
        while chunks:
            hand_on(chunks.pop(0))

    for copy in smalls[3:]:
        copy.wait()
    conv_gain = cg[...].reshape(1, width)

    def unfold(i, unit, odd):
        piece = att_all[i, unit].astype(f32)
        turned = swap_halves(piece)
        return jnp.concatenate([turned, piece] if odd else [piece, turned], axis=0)

    s_copies = {}

    def project_out(rec):
        gathered = jnp.concatenate(
            [
                jnp.where(
                    low, unfold(i, rec * heads + 2 * p, False), unfold(i, rec * heads + 2 * p + 1, True)
                ).astype(bf16)
                for i in range(nx)
                for p in range(pairs)
            ],
            axis=1,
        )
        parts[rec] = jnp.dot(
            gathered, wo[...].reshape(nx * pairs * LANES, width), preferred_element_type=f32
        ).astype(bf16)
        s_copies[rec] = remote(parts.at[rec], sibs.at[rec], ss.at[rec], sr.at[rec], sibling)
        s_copies[rec].start()

    first_frame = c * frames
    frame_ids = first_frame + lax.broadcasted_iota(jnp.int32, (frames, 1), 0)

    def up(rec):
        return remote(
            gb.at[rec, frames - RIM : frames, :], halo.at[0, rec], hs.at[0, rec], hr.at[0, rec],
            {"ctx": lax.rem(c + 1, n)},
        )

    def down(rec):
        return remote(
            gb.at[rec, 0:RIM, :], halo.at[1, rec], hs.at[1, rec], hr.at[1, rec], {"ctx": lax.rem(c + n - 1, n)}
        )


    def gate(rec):
        s_copies[rec].wait_recv()

        def strip(i, carry):
            near = pl.ds(pl.multiple_of(i * 32, 32), 32)
            at = pl.ds(pl.multiple_of(rec * frames + i * 32, 32), 32)
            total = feat[at, :].astype(f32) + (parts[rec, near, :].astype(f32) + sibs[rec, near, :].astype(f32))
            res[at, :] = total
            xn[at, :] = normalise(total, conv_gain)
            return carry

        lax.fori_loop(0, frames // 32, strip, 0, unroll=2)
        value_half = jnp.dot(xn[rows_of(rec), :], wglu[0], preferred_element_type=f32)
        gate_half = jnp.dot(xn[rows_of(rec), :], wglu[1], preferred_element_type=f32)
        gated = value_half * jax.nn.sigmoid(gate_half)
        kept = jnp.where(frame_ids < counts[rec], gated, 0.0).astype(bf16)
        gb[rec] = kept
        gp[rec, RIM : RIM + frames, :] = kept.astype(f32)

        @pl.when(c < n - 1)
        def _():
            up(rec).start()

        @pl.when(c > 0)
        def _():
            down(rec).start()

    def depthwise(rec):
        def channels(at, size):
            total = jnp.zeros((frames, size), f32)
            for tap in range(taps):
                begin = tap + RIM - taps // 2
                total = total + gp[rec, begin : begin + frames, at] * ker[tap : tap + 1, at]
            v = total * bns[at].reshape(1, size) + bnb[at].reshape(1, size)
            act[rec, :, at] = (v * jax.nn.sigmoid(v)).astype(bf16)

        def step(j, carry):
            channels(pl.ds(pl.multiple_of(j * LANES, LANES), LANES), LANES)
            return carry

        lax.fori_loop(0, chans // LANES, step, 0)
        if chans % LANES:
            channels(pl.ds(chans - chans % LANES, chans % LANES), chans % LANES)

    def rim(rec):
        @pl.when(c > 0)
        def _():
            up(rec).wait_recv()

        @pl.when(c == 0)
        def _():
            halo[0, rec] = jnp.zeros(halo.shape[2:], bf16)

        @pl.when(c < n - 1)
        def _():
            down(rec).wait_recv()

        @pl.when(c == n - 1)
        def _():
            halo[1, rec] = jnp.zeros(halo.shape[2:], bf16)

        gp[rec, 0:RIM, :] = halo[0, rec].astype(f32)
        gp[rec, RIM + frames : 2 * RIM + frames, :] = halo[1, rec].astype(f32)
        depthwise(rec)

    b_copies = []
    e_copies = []

    def pass_on(rec):
        b_copies[rec].wait_recv()
        for i in range(nx):
            sum5[rec, i] = (p5[rec, i, core].astype(f32) + s5[rec, i].astype(f32)).astype(bf16)
        for k in range(1, nx):
            copy = remote(sum5.at[rec, lax.rem(x + k, nx)], x5.at[rec, k], es.at[rec, k], er.at[rec, k], x_peer(k))
            copy.start()
            e_copies.append(copy)

    loads[5].wait()
    loads[3].wait()
    for copy in y_copies:
        copy.wait_recv()
    early = list(range((phases - 1) * per_phase))
    late = list(range((phases - 1) * per_phase, recs))
    for f in range(phases - 1):
        for copy in f_copies[f]:
            copy.wait_recv()
    for rec in early:
        project_out(rec)
    forward(phases - 1)
    for rec in early:
        gate(rec)
    for copy in f_copies[phases - 1]:
        copy.wait_recv()
    for rec in late:
        project_out(rec)
    for rec in late:
        gate(rec)
    loads[4].wait()
    for rec in range(recs):
        rim(rec)
        if rec > 0:
            pass_on(rec - 1)
        made = jnp.dot(act[rec], wpw[...], preferred_element_type=f32)
        p5[rec] = made.reshape(nx, 2, rm, width).astype(bf16)
        copy = remote(p5.at[rec, :, 1 - core], s5.at[rec], bs.at[rec], br.at[rec], sibling)
        copy.start()
        b_copies.append(copy)
    pass_on(recs - 1)

    row_start = pl.multiple_of(m * rm, rm)
    mine_ids = first_frame + row_start + lax.broadcasted_iota(jnp.int32, (rm, 1), 0)
    bound = clip[...].reshape(1, width).astype(f32) / 16.0
    for rec in range(recs):
        for k in range(1, nx):
            e_copies[rec * (nx - 1) + k - 1].wait_recv()
        at = pl.ds(pl.multiple_of(rec * frames + row_start, rm), rm)
        total = res[at, :] + sum5[rec, x].astype(f32)
        for k in range(1, nx):
            total = total + x5[rec, k].astype(f32)
        clipped = jnp.minimum(jnp.maximum(total, -bound), bound)
        out[rec] = jnp.where(mine_ids < counts[rec], clipped, 0.0).astype(bf16)

    waiting = list(w_copies.values()) + y_copies + list(s_copies.values()) + b_copies + e_copies
    for group in qk_copies + v_copies + z_copies + f_copies:
        waiting = waiting + group
    for copy in waiting:
        copy.wait_send()
    for rec in range(recs):
        @pl.when(c < n - 1)
        def _(rec=rec):
            up(rec).wait_send()

        @pl.when(c > 0)
        def _(rec=rec):
            down(rec).wait_send()


def shards(n, mp, ng, features, frame_counts, attn_gain, w_qkv, w_out, conv_gain, w_glu, kernel, bn_scale, bn_shift, w_pw, clip_level):
    recs, frames, width = features.shape
    nx = mp // 2
    rows = recs * frames
    local = w_qkv.shape[2]
    units = recs * local // HEAD_DIM
    phases = units // n
    half = frames // 2
    chans = w_glu.shape[2]
    rm = frames // mp
    taps = kernel.shape[0]
    vmem = pl.BlockSpec(memory_space=pltpu.VMEM)
    hbm = pl.BlockSpec(memory_space=pl.ANY)
    dma = pltpu.SemaphoreType.DMA
    slots = n // 2 if n <= 4 else 1
    scratch = [
        pltpu.VMEM((rows, width), bf16),
        pltpu.SMEM(frame_counts.shape, jnp.int32),
        pltpu.VMEM(attn_gain.shape, f32),
        pltpu.VMEM(conv_gain.shape, f32),
        pltpu.VMEM(kernel.shape, f32),
        pltpu.VMEM(bn_scale.shape, f32),
        pltpu.VMEM(bn_shift.shape, f32),
        pltpu.VMEM(clip_level.shape, jnp.int32),
        pltpu.VMEM(w_qkv.shape, bf16),
        pltpu.VMEM((nx, local, width), bf16),
        pltpu.VMEM(w_glu.shape, bf16),
        pltpu.VMEM(w_pw.shape, bf16),
        pltpu.VMEM((rows, width), bf16),
        pltpu.VMEM((units, frames, LANES), bf16),
        pltpu.VMEM((units, half, LANES), bf16),
        pltpu.VMEM((phases, n, frames, LANES), bf16),
        pltpu.VMEM((phases, n, half, LANES), bf16),
        pltpu.VMEM((phases, n, half, LANES), bf16),
        pltpu.VMEM((nx, units, half, LANES), bf16),
        pltpu.VMEM((slots, 2 * frames, n * frames), bf16),
        pltpu.VMEM((slots, 2 * frames, 1), f32),
        pltpu.VMEM((recs, frames, width), bf16),
        pltpu.VMEM((recs, frames, width), bf16),
        pltpu.VMEM((rows, width), f32),
        pltpu.VMEM((recs, frames, chans), bf16),
        pltpu.VMEM((recs, frames + 2 * RIM, chans), f32),
        pltpu.VMEM((2, recs, RIM, chans), bf16),
        pltpu.VMEM((recs, frames, chans), bf16),
        pltpu.VMEM((recs, nx, 2, rm, width), bf16),
        pltpu.VMEM((recs, nx, rm, width), bf16),
        pltpu.VMEM((recs, nx, rm, width), bf16),
        pltpu.VMEM((recs, nx, rm, width), bf16),
        dma((6,)),
        dma((8,)),
        dma((phases, n)), dma((phases, n)),
        dma((phases, n)), dma((phases, n)),
        dma((nx, W_CHUNKS)), dma((nx, W_CHUNKS)),
        dma((nx, W_CHUNKS, ng)), dma((nx, W_CHUNKS, ng)),
        dma((phases, n)), dma((phases, n)),
        dma((nx, phases, n)), dma((nx, phases, n)),
        dma((recs,)), dma((recs,)),
        dma((2, recs)), dma((2, recs)),
        dma((recs,)), dma((recs,)),
        dma((recs, nx)), dma((recs, nx)),
    ]
    return pl.pallas_call(
        functools.partial(fused, n, nx, ng, recs, frames, taps),
        out_shape=jax.ShapeDtypeStruct((recs, rm, width), bf16),
        in_specs=[hbm] * 12,
        out_specs=vmem,
        scratch_shapes=scratch,
        compiler_params=pltpu.CompilerParams(
            collective_id=0, has_side_effects=True, vmem_limit_bytes=56 * 2**20
        ),
    )(
        features.reshape(rows, width), frame_counts, attn_gain, w_qkv, w_out, conv_gain, w_glu, kernel,
        bn_scale, bn_shift, w_pw, clip_level,
    )


def solution(mesh):
    return jax.shard_map(
        functools.partial(shards, mesh.shape["ctx"], mesh.shape["mp"], mesh.shape["groups"]),
        mesh=mesh,
        in_specs=(
            P("groups", "ctx", None),
            P("groups"),
            P(),
            P(None, None, "mp"),
            P("mp", None),
            P(),
            P(None, None, "mp"),
            P(None, "mp"),
            P("mp"),
            P("mp"),
            P("mp", None),
            P(),
        ),
        out_specs=P("groups", ("ctx", "mp"), None),
        check_vma=False,
    )
```

```python
import functools

import jax
import jax.numpy as jnp
from jax import lax
from jax.experimental import pallas as pl
from jax.experimental.pallas import tpu as pltpu
from jax.sharding import PartitionSpec as P

MESH = pl.DeviceIdType.MESH
HEAD_DIM = 64
LANES = 128
RIM = 16
W_CHUNKS = 2
epsilon = 1e-05
masked_score = -1e30
f32 = jnp.float32
bf16 = jnp.bfloat16


def loop(count, step):
    if count <= 2:
        for i in range(count):
            step(i)
    else:
        lax.fori_loop(0, count, lambda i, carry: (step(i), carry)[1], 0)


def when(cond):
    if cond is True:
        return lambda f: f()
    return lambda f: pl.when(cond)(lambda: f())


def normalise(values, gain):
    centred = values - jnp.mean(values, axis=-1, keepdims=True)
    variance = jnp.mean(centred * centred, axis=-1, keepdims=True)
    return (centred * lax.rsqrt(variance + epsilon) * gain).astype(bf16)


def fused(
    n, nx, ng, recs, frames, taps,
    feat_h, counts_h, ag_h, wqkv_h, wout_h, cg_h, wglu_h, ker_h, bns_h, bnb_h, wpw_h, clip_h, out, least, most,
    feat, counts, ag, cg, ker, bns, bnb, clip,
    wqkv, wo, wglu, wpw, xn, qkv_s, qkv_r, atto, att_all, w_s, tot_s, parts, sibs, res, gb, gp, halo, act,
    p5, s5, sum5, x5,
    ld, sm, qs, qr, wos, wor, ys, yr, zs, zr, fs, fr, ss, sr, hs, hr, bs, br, es, er,
):
    c = lax.axis_index("ctx")
    m = lax.axis_index("mp")
    x = lax.div(m, 2)
    core = lax.rem(m, 2)
    g_rank = lax.axis_index("groups")
    sibling = {"mp": x * 2 + (1 - core)}
    rows, width = feat.shape
    pairs = wqkv.shape[2] // LANES
    units = recs * pairs
    chans = gb.shape[2]
    rm = frames // (2 * nx)
    group = min(recs, 2)
    block = group * frames

    def ctx_at(k):
        return lax.rem(c + k, n)

    def has_unit(rank):
        return True if units == n else rank < units

    def x_peer(k):
        return {"mp": lax.rem(x + k, nx) * 2 + core}

    def y_peer(k):
        return {"groups": lax.rem(g_rank + k, ng)}

    def remote(src, dst, send, recv, where):
        return pltpu.make_async_remote_copy(
            src_ref=src, dst_ref=dst, send_sem=send, recv_sem=recv, device_id=where, device_id_type=MESH
        )

    barrier = pltpu.get_barrier_semaphore()
    for k in range(1, n):
        pl.semaphore_signal(barrier, inc=1, device_id={"ctx": ctx_at(k)}, device_id_type=MESH)
    for k in range(1, nx):
        pl.semaphore_signal(barrier, inc=1, device_id=x_peer(k), device_id_type=MESH)
    for k in range(1, ng):
        pl.semaphore_signal(barrier, inc=1, device_id=y_peer(k), device_id_type=MESH)
    pl.semaphore_signal(barrier, inc=1, device_id=sibling, device_id_type=MESH)

    pairs_in = [(feat_h, feat), (ag_h, ag), (counts_h, counts), (cg_h, cg), (ker_h, ker), (bns_h, bns),
                (bnb_h, bnb), (clip_h, clip)]
    smalls = [pltpu.make_async_copy(src, dst, sm.at[i]) for i, (src, dst) in enumerate(pairs_in)]
    loads = [pltpu.make_async_copy(wqkv_h.at[i], wqkv.at[i], ld.at[i]) for i in range(3)]
    loads.append(pltpu.make_async_copy(wglu_h, wglu, ld.at[3]))
    loads.append(pltpu.make_async_copy(wpw_h, wpw, ld.at[4]))
    loads.append(pltpu.make_async_copy(wout_h, wo.at[x], ld.at[5]))
    smalls[0].start()
    smalls[1].start()
    for i in (1, 0, 2):
        loads[i].start()
    for copy in smalls[2:]:
        copy.start()
    smalls[0].wait()
    smalls[1].wait()

    gain = ag[...].reshape(1, width)

    def norm_in(i):
        at = pl.ds(pl.multiple_of(i * 32, 32), 32)
        xn[at, :] = normalise(feat[at, :].astype(f32), gain)

    lax.fori_loop(0, rows // 32, lambda i, carry: (norm_in(i), carry)[1], 0, unroll=4)

    pl.semaphore_wait(barrier, n - 1 + nx - 1 + ng - 1 + 1)

    local = wo.shape[1]
    share = local // ng
    sub = share // W_CHUNKS

    def w_rows(rank, chunk):
        return pl.ds(pl.multiple_of(rank * share + chunk * sub, sub), sub)

    w_copies = {}
    for chunk in range(W_CHUNKS):
        for k in range(1, nx):
            at = w_rows(g_rank, chunk)
            copy = remote(wout_h.at[at, :], wo.at[x, at, :], wos.at[k, chunk], wor.at[k, chunk], x_peer(k))
            copy.start()
            w_copies[k, chunk] = copy
    y_copies = []

    def hand_on(chunk):
        for k in range(1, nx):
            w_copies[k, chunk].wait_recv()
            at = w_rows(g_rank, chunk)
            held = wo.at[lax.rem(x - k + nx, nx), at, :]
            for j in range(1, ng):
                copy = remote(held, held, ys.at[k, chunk, j], yr.at[k, chunk, j], y_peer(j))
                copy.start()
                y_copies.append(copy)

    q_copies = []
    for i in (1, 0, 2):
        loads[i].wait()

        def project(g, i=i):
            at = pl.ds(pl.multiple_of(g * block, block), block)
            made = jnp.dot(xn[at, :], wqkv[i], preferred_element_type=f32).astype(bf16)
            for r in range(group):
                for p in range(pairs):
                    piece = made[r * frames : (r + 1) * frames, p * LANES : (p + 1) * LANES]
                    qkv_s[(g * group + r) * pairs + p, i] = piece

        loop(recs // group, project)
        for k in range(1, n):
            dest = ctx_at(k)
            copy = remote(
                qkv_s.at[lax.rem(dest, units), i], qkv_r.at[c, i], qs.at[i, k], qr.at[i, k], {"ctx": dest}
            )
            when(has_unit(dest))(copy.start)
            q_copies.append((copy, dest, i))

        @when(has_unit(c))
        def _(i=i):
            qkv_r[c, i] = qkv_s[lax.rem(c, units), i]

    z_copies = [
        remote(atto.at[k], att_all.at[x, lax.rem(c, units)], zs.at[k], zr.at[k], {"ctx": ctx_at(k)})
        for k in range(1, n)
    ]

    for i in (5, 3, 4):
        loads[i].start()
    hand_on(0)
    smalls[2].wait()

    def arrived(which):
        @when(has_unit(c))
        def _():
            for copy, _dest, i in q_copies:
                if i in which:
                    copy.wait_recv()

    arrived((1, 0))
    own_rec = lax.div(lax.rem(c, units), pairs)
    live_keys = counts[own_rec]
    key_count = n * frames
    lane = lax.broadcasted_iota(jnp.int32, (1, LANES), 1)
    low = lane < HEAD_DIM
    seen = lax.broadcasted_iota(jnp.int32, (1, key_count), 1) < live_keys
    slots = w_s.shape[0]

    def weigh(k0, slot):
        keys = qkv_r[:, 1].reshape(key_count, LANES)
        queries = jnp.concatenate([qkv_r[ctx_at(k0), 0], qkv_r[ctx_at(k0 + 1), 0]], axis=0)
        for h in range(2):
            mine = jnp.where(low if h == 0 else jnp.logical_not(low), queries, jnp.zeros((), bf16))
            scores = lax.dot_general(mine, keys, (((1,), (1,)), ((), ())), preferred_element_type=f32)
            scores = jnp.where(seen, scores, masked_score)
            top = jnp.max(scores, axis=-1, keepdims=True)
            weights = jnp.exp((scores - top) * (HEAD_DIM**-0.5))
            tot_s[slot, h] = jnp.sum(weights, axis=-1, keepdims=True)
            w_s[slot, h] = weights.astype(bf16)

    def mix(k0, slot):
        values = qkv_r[:, 2].reshape(key_count, LANES)
        heads = [
            jnp.dot(w_s[slot, h], values, preferred_element_type=f32) / tot_s[slot, h] for h in range(2)
        ]
        both = jnp.where(low, heads[0], heads[1]).astype(bf16)
        atto[k0] = both[:frames]
        atto[k0 + 1] = both[frames:]

    def give(k):
        if k == 0:
            att_all[x, lax.rem(c, units)] = atto[0]
        else:
            z_copies[k - 1].start()

    starts = list(range(0, n, 2))
    if slots > 1:
        @when(has_unit(c))
        def _():
            for slot, k0 in enumerate(starts):
                weigh(k0, slot)

    for chunk in range(1, W_CHUNKS):
        hand_on(chunk)
    arrived((2,))

    @when(has_unit(c))
    def _():
        if slots > 1:
            for slot, k0 in reversed(list(enumerate(starts))):
                mix(k0, slot)
                give(k0 + 1)
                give(k0)
        else:
            def whole_step(i, carry):
                weigh(2 * i, 0)
                mix(2 * i, 0)
                return carry

            lax.fori_loop(0, n // 2, whole_step, 0)
            for k in range(n):
                give(k)

    f_copies = []
    for k in [0] + list(range(n - 1, 0, -1)):
        unit = lax.rem(c - k + n, n)
        spot = lax.rem(unit, units)

        @when(has_unit(unit))
        def _(k=k, unit=unit, spot=spot):
            if k > 0:
                remote(atto.at[k], att_all.at[x, spot], zs.at[k], zr.at[k], {"ctx": unit}).wait_recv()
            for j in range(1, nx):
                remote(
                    att_all.at[x, spot], att_all.at[x, spot], fs.at[j, k], fr.at[j, k], x_peer(j)
                ).start()

        for j in range(1, nx):
            f_copies.append(
                (remote(att_all.at[x, spot], att_all.at[x, spot], fs.at[j, k], fr.at[j, k], x_peer(j)), unit)
            )

    loads[5].wait()
    for copy in y_copies:
        copy.wait_recv()
    for copy, unit in f_copies:
        when(has_unit(unit))(copy.wait_recv)

    s_copies = []
    for rec in range(recs):
        gathered = jnp.concatenate(
            [att_all[i, rec * pairs + p] for i in range(nx) for p in range(pairs)], axis=1
        )
        parts[rec] = jnp.dot(
            gathered, wo[...].reshape(nx * pairs * LANES, width), preferred_element_type=f32
        ).astype(bf16)
        copy = remote(parts.at[rec], sibs.at[rec], ss.at[rec], sr.at[rec], sibling)
        copy.start()
        s_copies.append(copy)

    smalls[3].wait()
    conv_gain = cg[...].reshape(1, width)
    for rec in range(recs):
        s_copies[rec].wait_recv()

        def norm_conv(i, rec=rec):
            near = pl.ds(pl.multiple_of(i * 32, 32), 32)
            at = pl.ds(pl.multiple_of(rec * frames + i * 32, 32), 32)
            total = feat[at, :].astype(f32) + (parts[rec, near, :].astype(f32) + sibs[rec, near, :].astype(f32))
            res[at, :] = total
            xn[at, :] = normalise(total, conv_gain)

        lax.fori_loop(0, frames // 32, lambda i, carry: (norm_conv(i), carry)[1], 0, unroll=4)

    loads[3].wait()
    first_frame = c * frames
    frame_ids = first_frame + lax.broadcasted_iota(jnp.int32, (frames, 1), 0)

    def gate(g):
        at = pl.ds(pl.multiple_of(g * block, block), block)
        value_half = jnp.dot(xn[at, :], wglu[0], preferred_element_type=f32)
        gate_half = jnp.dot(xn[at, :], wglu[1], preferred_element_type=f32)
        gated = value_half * jax.nn.sigmoid(gate_half)
        for r in range(group):
            rec = g * group + r
            kept = jnp.where(frame_ids < counts[rec], gated[r * frames : (r + 1) * frames], 0.0).astype(bf16)
            gb[rec] = kept
            gp[rec, RIM : RIM + frames, :] = kept.astype(f32)

    loop(recs // group, gate)

    def up():
        return remote(gb.at[:, frames - RIM : frames, :], halo.at[0], hs.at[0], hr.at[0], {"ctx": lax.rem(c + 1, n)})

    def down():
        return remote(gb.at[:, 0:RIM, :], halo.at[1], hs.at[1], hr.at[1], {"ctx": lax.rem(c + n - 1, n)})

    @pl.when(c < n - 1)
    def _():
        up().start()

    @pl.when(c > 0)
    def _():
        down().start()

    for copy in smalls[4:]:
        copy.wait()
    bound = clip[...].astype(f32) / 16.0
    least[...] = -bound
    most[...] = bound
    scale = bns[...].reshape(1, chans)
    shift = bnb[...].reshape(1, chans)

    def depthwise(rec, start, count):
        for lo in range(0, chans, LANES):
            hi = min(lo + LANES, chans)
            total = jnp.zeros((count, hi - lo), f32)
            for tap in range(taps):
                begin = start + tap + RIM - taps // 2
                total = total + gp[rec, begin : begin + count, lo:hi] * ker[tap : tap + 1, lo:hi]
            v = total * scale[:, lo:hi] + shift[:, lo:hi]
            act[rec, start : start + count, lo:hi] = (v * jax.nn.sigmoid(v)).astype(bf16)

    def rim():
        @pl.when(c > 0)
        def _():
            up().wait_recv()

        @pl.when(c == 0)
        def _():
            halo[0] = jnp.zeros(halo.shape[1:], bf16)

        @pl.when(c < n - 1)
        def _():
            down().wait_recv()

        @pl.when(c == n - 1)
        def _():
            halo[1] = jnp.zeros(halo.shape[1:], bf16)

    b_copies = []
    e_copies = []

    def pass_on(rec):
        b_copies[rec].wait_recv()
        for i in range(nx):
            sum5[rec, i] = (p5[rec, i, core].astype(f32) + s5[rec, i].astype(f32)).astype(bf16)
        for k in range(1, nx):
            copy = remote(sum5.at[rec, lax.rem(x + k, nx)], x5.at[rec, k], es.at[rec, k], er.at[rec, k], x_peer(k))
            copy.start()
            e_copies.append(copy)

    for rec in range(recs):
        depthwise(rec, RIM, frames - 2 * RIM)
        if rec == 0:
            rim()
            loads[4].wait()
        gp[rec, 0:RIM, :] = halo[0, rec].astype(f32)
        gp[rec, RIM + frames : 2 * RIM + frames, :] = halo[1, rec].astype(f32)
        depthwise(rec, 0, RIM)
        depthwise(rec, frames - RIM, RIM)
        if rec > 0:
            pass_on(rec - 1)
        made = jnp.dot(act[rec], wpw[...], preferred_element_type=f32)
        p5[rec] = made.reshape(nx, 2, rm, width).astype(bf16)
        copy = remote(p5.at[rec, :, 1 - core], s5.at[rec], bs.at[rec], br.at[rec], sibling)
        copy.start()
        b_copies.append(copy)
    pass_on(recs - 1)

    row_start = pl.multiple_of(m * rm, rm)
    mine_ids = first_frame + row_start + lax.broadcasted_iota(jnp.int32, (rm, 1), 0)
    for rec in range(recs):
        for k in range(1, nx):
            e_copies[rec * (nx - 1) + k - 1].wait_recv()
        at = pl.ds(pl.multiple_of(rec * frames + row_start, rm), rm)
        total = res[at, :] + sum5[rec, x].astype(f32)
        for k in range(1, nx):
            total = total + x5[rec, k].astype(f32)
        out[rec] = jnp.where(mine_ids < counts[rec], total, 0.0).astype(bf16)

    for copy, dest, _i in q_copies:
        when(has_unit(dest))(copy.wait_send)

    @when(has_unit(c))
    def _():
        for copy in z_copies:
            copy.wait_send()

    for copy, unit in f_copies:
        when(has_unit(unit))(copy.wait_send)
    for copy in list(w_copies.values()) + y_copies + s_copies + b_copies + e_copies:
        copy.wait_send()

    @pl.when(c < n - 1)
    def _():
        up().wait_send()

    @pl.when(c > 0)
    def _():
        down().wait_send()


def shards(n, mp, ng, features, frame_counts, attn_gain, w_qkv, w_out, conv_gain, w_glu, kernel, bn_scale, bn_shift, w_pw, clip_level):
    recs, frames, width = features.shape
    nx = mp // 2
    rows = recs * frames
    local = w_qkv.shape[2]
    units = recs * local // LANES
    chans = w_glu.shape[2]
    rm = frames // mp
    taps = kernel.shape[0]
    vmem = pl.BlockSpec(memory_space=pltpu.VMEM)
    hbm = pl.BlockSpec(memory_space=pl.ANY)
    dma = pltpu.SemaphoreType.DMA
    slots = n // 2 if n <= 4 else 1
    scratch = [
        pltpu.VMEM((rows, width), bf16),
        pltpu.SMEM(frame_counts.shape, jnp.int32),
        pltpu.VMEM(attn_gain.shape, f32),
        pltpu.VMEM(conv_gain.shape, f32),
        pltpu.VMEM(kernel.shape, f32),
        pltpu.VMEM(bn_scale.shape, f32),
        pltpu.VMEM(bn_shift.shape, f32),
        pltpu.VMEM(clip_level.shape, jnp.int32),
        pltpu.VMEM(w_qkv.shape, bf16),
        pltpu.VMEM((nx, local, width), bf16),
        pltpu.VMEM(w_glu.shape, bf16),
        pltpu.VMEM(w_pw.shape, bf16),
        pltpu.VMEM((rows, width), bf16),
        pltpu.VMEM((units, 3, frames, LANES), bf16),
        pltpu.VMEM((n, 3, frames, LANES), bf16),
        pltpu.VMEM((n, frames, LANES), bf16),
        pltpu.VMEM((nx, units, frames, LANES), bf16),
        pltpu.VMEM((slots, 2, 2 * frames, n * frames), bf16),
        pltpu.VMEM((slots, 2, 2 * frames, 1), f32),
        pltpu.VMEM((recs, frames, width), bf16),
        pltpu.VMEM((recs, frames, width), bf16),
        pltpu.VMEM((rows, width), f32),
        pltpu.VMEM((recs, frames, chans), bf16),
        pltpu.VMEM((recs, frames + 2 * RIM, chans), f32),
        pltpu.VMEM((2, recs, RIM, chans), bf16),
        pltpu.VMEM((recs, frames, chans), bf16),
        pltpu.VMEM((recs, nx, 2, rm, width), bf16),
        pltpu.VMEM((recs, nx, rm, width), bf16),
        pltpu.VMEM((recs, nx, rm, width), bf16),
        pltpu.VMEM((recs, nx, rm, width), bf16),
        dma((6,)),
        dma((8,)),
        dma((3, n)), dma((3, n)),
        dma((nx, W_CHUNKS)), dma((nx, W_CHUNKS)),
        dma((nx, W_CHUNKS, ng)), dma((nx, W_CHUNKS, ng)),
        dma((n,)), dma((n,)),
        dma((nx, n)), dma((nx, n)),
        dma((recs,)), dma((recs,)),
        dma((2,)), dma((2,)),
        dma((recs,)), dma((recs,)),
        dma((recs, nx)), dma((recs, nx)),
    ]
    summed, least, most = pl.pallas_call(
        functools.partial(fused, n, nx, ng, recs, frames, taps),
        out_shape=(
            jax.ShapeDtypeStruct((recs, rm, width), bf16),
            jax.ShapeDtypeStruct((width,), f32),
            jax.ShapeDtypeStruct((width,), f32),
        ),
        in_specs=[hbm] * 12,
        out_specs=(vmem, vmem, vmem),
        scratch_shapes=scratch,
        compiler_params=pltpu.CompilerParams(
            collective_id=0, has_side_effects=True, vmem_limit_bytes=56 * 2**20
        ),
    )(
        features.reshape(rows, width), frame_counts, attn_gain, w_qkv, w_out, conv_gain, w_glu, kernel,
        bn_scale, bn_shift, w_pw, clip_level,
    )
    return jnp.clip(summed.astype(f32), least, most).astype(bf16)


def solution(mesh):
    return jax.shard_map(
        functools.partial(shards, mesh.shape["ctx"], mesh.shape["mp"], mesh.shape["groups"]),
        mesh=mesh,
        in_specs=(
            P("groups", "ctx", None),
            P("groups"),
            P(),
            P(None, None, "mp"),
            P("mp", None),
            P(),
            P(None, None, "mp"),
            P(None, "mp"),
            P("mp"),
            P("mp"),
            P("mp", None),
            P(),
        ),
        out_specs=P("groups", ("ctx", "mp"), None),
        check_vma=False,
    )
```

```python
import functools

import jax
import jax.numpy as jnp
from jax import lax
from jax.experimental import pallas as pl
from jax.experimental.pallas import tpu as pltpu
from jax.sharding import PartitionSpec as P

MESH = pl.DeviceIdType.MESH
HEAD_DIM = 64
LANES = 128
RIM = 16
W_CHUNKS = 4
epsilon = 1e-05
masked_score = -1e30
f32 = jnp.float32
bf16 = jnp.bfloat16


def loop(count, step):
    if count <= 2:
        for i in range(count):
            step(i)
    else:
        lax.fori_loop(0, count, lambda i, carry: (step(i), carry)[1], 0)


def when(cond):
    if cond is True:
        return lambda f: f()
    return lambda f: pl.when(cond)(lambda: f())


def normalise(values, gain):
    centred = values - jnp.mean(values, axis=-1, keepdims=True)
    variance = jnp.mean(centred * centred, axis=-1, keepdims=True)
    return (centred * lax.rsqrt(variance + epsilon) * gain).astype(bf16)


def fused(
    n, nx, ng, recs, frames, taps,
    feat_h, counts_h, ag_h, wqkv_h, wout_h, cg_h, wglu_h, ker_h, bns_h, bnb_h, wpw_h, clip_h, out, least, most,
    feat, counts, ag, cg, ker, bns, bnb, clip,
    wqkv, wo, wglu, wpw, xn, qkv_s, qkv_r, atto, att_all, w_s, tot_s, parts, sibs, res, gb, gp, halo, act,
    p5, s5, sum5, x5,
    ld, sm, qs, qr, wos, wor, ys, yr, zs, zr, fs, fr, ss, sr, hs, hr, bs, br, es, er,
):
    c = lax.axis_index("ctx")
    m = lax.axis_index("mp")
    x = lax.div(m, 2)
    core = lax.rem(m, 2)
    g_rank = lax.axis_index("groups")
    sibling = {"mp": x * 2 + (1 - core)}
    rows, width = feat.shape
    pairs = wqkv.shape[2] // LANES
    units = recs * pairs
    chans = gb.shape[2]
    rm = frames // (2 * nx)
    group = min(recs, 2)
    block = group * frames

    def ctx_at(k):
        return lax.rem(c + k, n)

    def has_unit(rank):
        return True if units == n else rank < units

    def x_peer(k):
        return {"mp": lax.rem(x + k, nx) * 2 + core}

    def y_peer(k):
        return {"groups": lax.rem(g_rank + k, ng)}

    def remote(src, dst, send, recv, where):
        return pltpu.make_async_remote_copy(
            src_ref=src, dst_ref=dst, send_sem=send, recv_sem=recv, device_id=where, device_id_type=MESH
        )

    barrier = pltpu.get_barrier_semaphore()
    for k in range(1, n):
        pl.semaphore_signal(barrier, inc=1, device_id={"ctx": ctx_at(k)}, device_id_type=MESH)
    for k in range(1, nx):
        pl.semaphore_signal(barrier, inc=1, device_id=x_peer(k), device_id_type=MESH)
    for k in range(1, ng):
        pl.semaphore_signal(barrier, inc=1, device_id=y_peer(k), device_id_type=MESH)
    pl.semaphore_signal(barrier, inc=1, device_id=sibling, device_id_type=MESH)

    pairs_in = [(feat_h, feat), (ag_h, ag), (counts_h, counts), (cg_h, cg), (ker_h, ker), (bns_h, bns),
                (bnb_h, bnb), (clip_h, clip)]
    smalls = [pltpu.make_async_copy(src, dst, sm.at[i]) for i, (src, dst) in enumerate(pairs_in)]
    loads = [pltpu.make_async_copy(wqkv_h.at[i], wqkv.at[i], ld.at[i]) for i in range(3)]
    loads.append(pltpu.make_async_copy(wglu_h, wglu, ld.at[3]))
    loads.append(pltpu.make_async_copy(wpw_h, wpw, ld.at[4]))
    loads.append(pltpu.make_async_copy(wout_h, wo.at[x], ld.at[5]))
    smalls[0].start()
    smalls[1].start()
    for i in (1, 0, 2):
        loads[i].start()
    for copy in smalls[2:]:
        copy.start()
    smalls[0].wait()
    smalls[1].wait()

    gain = ag[...].reshape(1, width)

    def norm_in(i):
        at = pl.ds(pl.multiple_of(i * 32, 32), 32)
        xn[at, :] = normalise(feat[at, :].astype(f32), gain)

    lax.fori_loop(0, rows // 32, lambda i, carry: (norm_in(i), carry)[1], 0, unroll=4)

    pl.semaphore_wait(barrier, n - 1 + nx - 1 + ng - 1 + 1)

    local = wo.shape[1]
    share = local // ng
    sub = share // W_CHUNKS

    def w_rows(rank, chunk):
        return pl.ds(pl.multiple_of(rank * share + chunk * sub, sub), sub)

    w_copies = {}
    for chunk in range(W_CHUNKS):
        for k in range(1, nx):
            at = w_rows(g_rank, chunk)
            copy = remote(wout_h.at[at, :], wo.at[x, at, :], wos.at[k, chunk], wor.at[k, chunk], x_peer(k))
            copy.start()
            w_copies[k, chunk] = copy
    y_copies = []

    def hand_on(chunk):
        for k in range(1, nx):
            w_copies[k, chunk].wait_recv()
            at = w_rows(g_rank, chunk)
            held = wo.at[lax.rem(x - k + nx, nx), at, :]
            for j in range(1, ng):
                copy = remote(held, held, ys.at[k, chunk, j], yr.at[k, chunk, j], y_peer(j))
                copy.start()
                y_copies.append(copy)

    q_copies = []
    for i in (1, 0, 2):
        loads[i].wait()

        def project(g, i=i):
            at = pl.ds(pl.multiple_of(g * block, block), block)
            made = jnp.dot(xn[at, :], wqkv[i], preferred_element_type=f32).astype(bf16)
            for r in range(group):
                for p in range(pairs):
                    piece = made[r * frames : (r + 1) * frames, p * LANES : (p + 1) * LANES]
                    qkv_s[(g * group + r) * pairs + p, i] = piece

        loop(recs // group, project)
        for k in range(1, n):
            dest = ctx_at(k)
            copy = remote(
                qkv_s.at[lax.rem(dest, units), i], qkv_r.at[c, i], qs.at[i, k], qr.at[i, k], {"ctx": dest}
            )
            when(has_unit(dest))(copy.start)
            q_copies.append((copy, dest, i))

        @when(has_unit(c))
        def _(i=i):
            qkv_r[c, i] = qkv_s[lax.rem(c, units), i]

    z_copies = [
        remote(atto.at[k], att_all.at[x, lax.rem(c, units)], zs.at[k], zr.at[k], {"ctx": ctx_at(k)})
        for k in range(1, n)
    ]

    for i in (5, 3, 4):
        loads[i].start()
    hand_on(0)
    hand_on(1)
    smalls[2].wait()

    def arrived(which):
        @when(has_unit(c))
        def _():
            for copy, _dest, i in q_copies:
                if i in which:
                    copy.wait_recv()

    arrived((1, 0))
    own_rec = lax.div(lax.rem(c, units), pairs)
    live_keys = counts[own_rec]
    key_count = n * frames
    lane = lax.broadcasted_iota(jnp.int32, (1, LANES), 1)
    low = lane < HEAD_DIM
    seen = lax.broadcasted_iota(jnp.int32, (1, key_count), 1) < live_keys
    slots = w_s.shape[0]

    def weigh(k0, slot):
        keys = qkv_r[:, 1].reshape(key_count, LANES)
        queries = jnp.concatenate([qkv_r[ctx_at(k0), 0], qkv_r[ctx_at(k0 + 1), 0]], axis=0)
        for h in range(2):
            mine = jnp.where(low if h == 0 else jnp.logical_not(low), queries, jnp.zeros((), bf16))
            scores = lax.dot_general(mine, keys, (((1,), (1,)), ((), ())), preferred_element_type=f32)
            scores = jnp.where(seen, scores, masked_score)
            top = jnp.max(scores, axis=-1, keepdims=True)
            weights = jnp.exp((scores - top) * (HEAD_DIM**-0.5))
            tot_s[slot, h] = jnp.sum(weights, axis=-1, keepdims=True)
            w_s[slot, h] = weights.astype(bf16)

    def mix(k0, slot):
        values = qkv_r[:, 2].reshape(key_count, LANES)
        heads = [
            jnp.dot(w_s[slot, h], values, preferred_element_type=f32) / tot_s[slot, h] for h in range(2)
        ]
        both = jnp.where(low, heads[0], heads[1]).astype(bf16)
        atto[k0] = both[:frames]
        atto[k0 + 1] = both[frames:]

    def give(k):
        if k == 0:
            att_all[x, lax.rem(c, units)] = atto[0]
        else:
            z_copies[k - 1].start()

    starts = list(range(0, n, 2))
    if slots > 1:
        @when(has_unit(c))
        def _():
            for slot, k0 in enumerate(starts):
                weigh(k0, slot)

    for chunk in range(2, W_CHUNKS):
        hand_on(chunk)
    arrived((2,))

    @when(has_unit(c))
    def _():
        if slots > 1:
            for slot, k0 in reversed(list(enumerate(starts))):
                mix(k0, slot)
                give(k0 + 1)
                give(k0)
        else:
            def whole_step(i, carry):
                weigh(2 * i, 0)
                mix(2 * i, 0)
                return carry

            lax.fori_loop(0, n // 2, whole_step, 0)
            for k in range(n):
                give(k)

    f_copies = []
    for k in [0] + list(range(n - 1, 0, -1)):
        unit = lax.rem(c - k + n, n)
        spot = lax.rem(unit, units)

        @when(has_unit(unit))
        def _(k=k, unit=unit, spot=spot):
            if k > 0:
                remote(atto.at[k], att_all.at[x, spot], zs.at[k], zr.at[k], {"ctx": unit}).wait_recv()
            for j in range(1, nx):
                remote(
                    att_all.at[x, spot], att_all.at[x, spot], fs.at[j, k], fr.at[j, k], x_peer(j)
                ).start()

        for j in range(1, nx):
            f_copies.append(
                (remote(att_all.at[x, spot], att_all.at[x, spot], fs.at[j, k], fr.at[j, k], x_peer(j)), unit)
            )

    loads[5].wait()
    for copy in y_copies:
        copy.wait_recv()
    for copy, unit in f_copies:
        when(has_unit(unit))(copy.wait_recv)

    s_copies = []
    for rec in range(recs):
        gathered = jnp.concatenate(
            [att_all[i, rec * pairs + p] for i in range(nx) for p in range(pairs)], axis=1
        )
        parts[rec] = jnp.dot(
            gathered, wo[...].reshape(nx * pairs * LANES, width), preferred_element_type=f32
        ).astype(bf16)
        copy = remote(parts.at[rec], sibs.at[rec], ss.at[rec], sr.at[rec], sibling)
        copy.start()
        s_copies.append(copy)

    smalls[3].wait()
    conv_gain = cg[...].reshape(1, width)
    for rec in range(recs):
        s_copies[rec].wait_recv()

        def norm_conv(i, rec=rec):
            near = pl.ds(pl.multiple_of(i * 32, 32), 32)
            at = pl.ds(pl.multiple_of(rec * frames + i * 32, 32), 32)
            total = feat[at, :].astype(f32) + (parts[rec, near, :].astype(f32) + sibs[rec, near, :].astype(f32))
            res[at, :] = total
            xn[at, :] = normalise(total, conv_gain)

        lax.fori_loop(0, frames // 32, lambda i, carry: (norm_conv(i), carry)[1], 0, unroll=4)

    loads[3].wait()
    first_frame = c * frames
    frame_ids = first_frame + lax.broadcasted_iota(jnp.int32, (frames, 1), 0)

    def gate(g):
        at = pl.ds(pl.multiple_of(g * block, block), block)
        value_half = jnp.dot(xn[at, :], wglu[0], preferred_element_type=f32)
        gate_half = jnp.dot(xn[at, :], wglu[1], preferred_element_type=f32)
        gated = value_half * jax.nn.sigmoid(gate_half)
        for r in range(group):
            rec = g * group + r
            kept = jnp.where(frame_ids < counts[rec], gated[r * frames : (r + 1) * frames], 0.0).astype(bf16)
            gb[rec] = kept
            gp[rec, RIM : RIM + frames, :] = kept.astype(f32)

    loop(recs // group, gate)

    def up():
        return remote(gb.at[:, frames - RIM : frames, :], halo.at[0], hs.at[0], hr.at[0], {"ctx": lax.rem(c + 1, n)})

    def down():
        return remote(gb.at[:, 0:RIM, :], halo.at[1], hs.at[1], hr.at[1], {"ctx": lax.rem(c + n - 1, n)})

    @pl.when(c < n - 1)
    def _():
        up().start()

    @pl.when(c > 0)
    def _():
        down().start()

    for copy in smalls[4:]:
        copy.wait()
    bound = clip[...].astype(f32) / 16.0
    least[...] = -bound
    most[...] = bound
    scale = bns[...].reshape(1, chans)
    shift = bnb[...].reshape(1, chans)

    def depthwise(rec, start, count):
        for lo in range(0, chans, LANES):
            hi = min(lo + LANES, chans)
            total = jnp.zeros((count, hi - lo), f32)
            for tap in range(taps):
                begin = start + tap + RIM - taps // 2
                total = total + gp[rec, begin : begin + count, lo:hi] * ker[tap : tap + 1, lo:hi]
            v = total * scale[:, lo:hi] + shift[:, lo:hi]
            act[rec, start : start + count, lo:hi] = (v * jax.nn.sigmoid(v)).astype(bf16)

    def rim():
        @pl.when(c > 0)
        def _():
            up().wait_recv()

        @pl.when(c == 0)
        def _():
            halo[0] = jnp.zeros(halo.shape[1:], bf16)

        @pl.when(c < n - 1)
        def _():
            down().wait_recv()

        @pl.when(c == n - 1)
        def _():
            halo[1] = jnp.zeros(halo.shape[1:], bf16)

    b_copies = []
    e_copies = []

    def pass_on(rec):
        b_copies[rec].wait_recv()
        for i in range(nx):
            sum5[rec, i] = (p5[rec, i, core].astype(f32) + s5[rec, i].astype(f32)).astype(bf16)
        for k in range(1, nx):
            copy = remote(sum5.at[rec, lax.rem(x + k, nx)], x5.at[rec, k], es.at[rec, k], er.at[rec, k], x_peer(k))
            copy.start()
            e_copies.append(copy)

    for rec in range(recs):
        if rec == 0:
            depthwise(rec, RIM, frames - 2 * RIM)
            rim()
            loads[4].wait()
        gp[rec, 0:RIM, :] = halo[0, rec].astype(f32)
        gp[rec, RIM + frames : 2 * RIM + frames, :] = halo[1, rec].astype(f32)
        if rec == 0:
            depthwise(rec, 0, RIM)
            depthwise(rec, frames - RIM, RIM)
        else:
            depthwise(rec, 0, frames // 2)
            pass_on(rec - 1)
            depthwise(rec, frames // 2, frames // 2)
        made = jnp.dot(act[rec], wpw[...], preferred_element_type=f32)
        p5[rec] = made.reshape(nx, 2, rm, width).astype(bf16)
        copy = remote(p5.at[rec, :, 1 - core], s5.at[rec], bs.at[rec], br.at[rec], sibling)
        copy.start()
        b_copies.append(copy)
    pass_on(recs - 1)

    row_start = pl.multiple_of(m * rm, rm)
    mine_ids = first_frame + row_start + lax.broadcasted_iota(jnp.int32, (rm, 1), 0)
    for rec in range(recs):
        for k in range(1, nx):
            e_copies[rec * (nx - 1) + k - 1].wait_recv()
        at = pl.ds(pl.multiple_of(rec * frames + row_start, rm), rm)
        total = res[at, :] + sum5[rec, x].astype(f32)
        for k in range(1, nx):
            total = total + x5[rec, k].astype(f32)
        out[rec] = jnp.where(mine_ids < counts[rec], total, 0.0).astype(bf16)

    for copy, dest, _i in q_copies:
        when(has_unit(dest))(copy.wait_send)

    @when(has_unit(c))
    def _():
        for copy in z_copies:
            copy.wait_send()

    for copy, unit in f_copies:
        when(has_unit(unit))(copy.wait_send)
    for copy in list(w_copies.values()) + y_copies + s_copies + b_copies + e_copies:
        copy.wait_send()

    @pl.when(c < n - 1)
    def _():
        up().wait_send()

    @pl.when(c > 0)
    def _():
        down().wait_send()


def shards(n, mp, ng, features, frame_counts, attn_gain, w_qkv, w_out, conv_gain, w_glu, kernel, bn_scale, bn_shift, w_pw, clip_level):
    recs, frames, width = features.shape
    nx = mp // 2
    rows = recs * frames
    local = w_qkv.shape[2]
    units = recs * local // LANES
    chans = w_glu.shape[2]
    rm = frames // mp
    taps = kernel.shape[0]
    vmem = pl.BlockSpec(memory_space=pltpu.VMEM)
    hbm = pl.BlockSpec(memory_space=pl.ANY)
    dma = pltpu.SemaphoreType.DMA
    slots = n // 2 if n <= 4 else 1
    scratch = [
        pltpu.VMEM((rows, width), bf16),
        pltpu.SMEM(frame_counts.shape, jnp.int32),
        pltpu.VMEM(attn_gain.shape, f32),
        pltpu.VMEM(conv_gain.shape, f32),
        pltpu.VMEM(kernel.shape, f32),
        pltpu.VMEM(bn_scale.shape, f32),
        pltpu.VMEM(bn_shift.shape, f32),
        pltpu.VMEM(clip_level.shape, jnp.int32),
        pltpu.VMEM(w_qkv.shape, bf16),
        pltpu.VMEM((nx, local, width), bf16),
        pltpu.VMEM(w_glu.shape, bf16),
        pltpu.VMEM(w_pw.shape, bf16),
        pltpu.VMEM((rows, width), bf16),
        pltpu.VMEM((units, 3, frames, LANES), bf16),
        pltpu.VMEM((n, 3, frames, LANES), bf16),
        pltpu.VMEM((n, frames, LANES), bf16),
        pltpu.VMEM((nx, units, frames, LANES), bf16),
        pltpu.VMEM((slots, 2, 2 * frames, n * frames), bf16),
        pltpu.VMEM((slots, 2, 2 * frames, 1), f32),
        pltpu.VMEM((recs, frames, width), bf16),
        pltpu.VMEM((recs, frames, width), bf16),
        pltpu.VMEM((rows, width), f32),
        pltpu.VMEM((recs, frames, chans), bf16),
        pltpu.VMEM((recs, frames + 2 * RIM, chans), f32),
        pltpu.VMEM((2, recs, RIM, chans), bf16),
        pltpu.VMEM((recs, frames, chans), bf16),
        pltpu.VMEM((recs, nx, 2, rm, width), bf16),
        pltpu.VMEM((recs, nx, rm, width), bf16),
        pltpu.VMEM((recs, nx, rm, width), bf16),
        pltpu.VMEM((recs, nx, rm, width), bf16),
        dma((6,)),
        dma((8,)),
        dma((3, n)), dma((3, n)),
        dma((nx, W_CHUNKS)), dma((nx, W_CHUNKS)),
        dma((nx, W_CHUNKS, ng)), dma((nx, W_CHUNKS, ng)),
        dma((n,)), dma((n,)),
        dma((nx, n)), dma((nx, n)),
        dma((recs,)), dma((recs,)),
        dma((2,)), dma((2,)),
        dma((recs,)), dma((recs,)),
        dma((recs, nx)), dma((recs, nx)),
    ]
    summed, least, most = pl.pallas_call(
        functools.partial(fused, n, nx, ng, recs, frames, taps),
        out_shape=(
            jax.ShapeDtypeStruct((recs, rm, width), bf16),
            jax.ShapeDtypeStruct((width,), f32),
            jax.ShapeDtypeStruct((width,), f32),
        ),
        in_specs=[hbm] * 12,
        out_specs=(vmem, vmem, vmem),
        scratch_shapes=scratch,
        compiler_params=pltpu.CompilerParams(
            collective_id=0, has_side_effects=True, vmem_limit_bytes=56 * 2**20
        ),
    )(
        features.reshape(rows, width), frame_counts, attn_gain, w_qkv, w_out, conv_gain, w_glu, kernel,
        bn_scale, bn_shift, w_pw, clip_level,
    )
    return jnp.clip(summed.astype(f32), least, most).astype(bf16)


def solution(mesh):
    return jax.shard_map(
        functools.partial(shards, mesh.shape["ctx"], mesh.shape["mp"], mesh.shape["groups"]),
        mesh=mesh,
        in_specs=(
            P("groups", "ctx", None),
            P("groups"),
            P(),
            P(None, None, "mp"),
            P("mp", None),
            P(),
            P(None, None, "mp"),
            P(None, "mp"),
            P("mp"),
            P("mp"),
            P("mp", None),
            P(),
        ),
        out_specs=P("groups", ("ctx", "mp"), None),
        check_vma=False,
    )
```

```python
import functools

import jax
import jax.numpy as jnp
from jax import lax
from jax.experimental import pallas as pl
from jax.experimental.pallas import tpu as pltpu
from jax.sharding import PartitionSpec as P

MESH = pl.DeviceIdType.MESH
HEAD_DIM = 64
LANES = 128
RIM = 16
W_CHUNKS = 4
epsilon = 1e-05
masked_score = -1e30
f32 = jnp.float32
bf16 = jnp.bfloat16


def loop(count, step):
    if count <= 2:
        for i in range(count):
            step(i)
    else:
        lax.fori_loop(0, count, lambda i, carry: (step(i), carry)[1], 0)


def when(cond):
    if cond is True:
        return lambda f: f()
    return lambda f: pl.when(cond)(lambda: f())


def normalise(values, gain):
    centred = values - jnp.mean(values, axis=-1, keepdims=True)
    variance = jnp.mean(centred * centred, axis=-1, keepdims=True)
    return (centred * lax.rsqrt(variance + epsilon) * gain).astype(bf16)


def fused(
    n, nx, ng, recs, frames, taps,
    feat_h, counts_h, ag_h, wqkv_h, wout_h, cg_h, wglu_h, ker_h, bns_h, bnb_h, wpw_h, clip_h, out, least, most,
    feat, counts, ag, cg, ker, bns, bnb, clip,
    wqkv, wo, wglu, wpw, xn, qkv_s, qkv_r, atto, att_all, w_s, tot_s, parts, sibs, res, gb, gp, halo, act,
    p5, s5, sum5, x5,
    ld, sm, qs, qr, wos, wor, ys, yr, zs, zr, fs, fr, ss, sr, hs, hr, bs, br, es, er,
):
    c = lax.axis_index("ctx")
    m = lax.axis_index("mp")
    x = lax.div(m, 2)
    core = lax.rem(m, 2)
    g_rank = lax.axis_index("groups")
    sibling = {"mp": x * 2 + (1 - core)}
    rows, width = feat.shape
    pairs = wqkv.shape[2] // LANES
    units = recs * pairs
    chans = gb.shape[2]
    rm = frames // (2 * nx)
    group = min(recs, 2)
    block = group * frames

    def ctx_at(k):
        return lax.rem(c + k, n)

    def has_unit(rank):
        return True if units == n else rank < units

    def x_peer(k):
        return {"mp": lax.rem(x + k, nx) * 2 + core}

    def y_peer(k):
        return {"groups": lax.rem(g_rank + k, ng)}

    def remote(src, dst, send, recv, where):
        return pltpu.make_async_remote_copy(
            src_ref=src, dst_ref=dst, send_sem=send, recv_sem=recv, device_id=where, device_id_type=MESH
        )

    barrier = pltpu.get_barrier_semaphore()
    for k in range(1, n):
        pl.semaphore_signal(barrier, inc=1, device_id={"ctx": ctx_at(k)}, device_id_type=MESH)
    for k in range(1, nx):
        pl.semaphore_signal(barrier, inc=1, device_id=x_peer(k), device_id_type=MESH)
    for k in range(1, ng):
        pl.semaphore_signal(barrier, inc=1, device_id=y_peer(k), device_id_type=MESH)
    pl.semaphore_signal(barrier, inc=1, device_id=sibling, device_id_type=MESH)

    pairs_in = [(feat_h, feat), (ag_h, ag), (counts_h, counts), (cg_h, cg), (ker_h, ker), (bns_h, bns),
                (bnb_h, bnb), (clip_h, clip)]
    smalls = [pltpu.make_async_copy(src, dst, sm.at[i]) for i, (src, dst) in enumerate(pairs_in)]
    loads = [pltpu.make_async_copy(wqkv_h.at[i], wqkv.at[i], ld.at[i]) for i in range(3)]
    loads.append(pltpu.make_async_copy(wglu_h, wglu, ld.at[3]))
    loads.append(pltpu.make_async_copy(wpw_h, wpw, ld.at[4]))
    loads.append(pltpu.make_async_copy(wout_h, wo.at[x], ld.at[5]))
    smalls[0].start()
    smalls[1].start()
    for i in (1, 0, 2):
        loads[i].start()
    for copy in smalls[2:]:
        copy.start()
    smalls[0].wait()
    smalls[1].wait()

    gain = ag[...].reshape(1, width)

    def norm_in(i):
        at = pl.ds(pl.multiple_of(i * 32, 32), 32)
        xn[at, :] = normalise(feat[at, :].astype(f32), gain)

    lax.fori_loop(0, rows // 32, lambda i, carry: (norm_in(i), carry)[1], 0, unroll=4)

    pl.semaphore_wait(barrier, n - 1 + nx - 1 + ng - 1 + 1)

    local = wo.shape[1]
    share = local // ng
    sub = share // W_CHUNKS

    def w_rows(rank, chunk):
        return pl.ds(pl.multiple_of(rank * share + chunk * sub, sub), sub)

    w_copies = {}
    for chunk in range(W_CHUNKS):
        for k in range(1, nx):
            at = w_rows(g_rank, chunk)
            copy = remote(wout_h.at[at, :], wo.at[x, at, :], wos.at[k, chunk], wor.at[k, chunk], x_peer(k))
            w_copies[k, chunk] = copy
    y_copies = []

    def hand_on(chunk):
        for k in range(1, nx):
            w_copies[k, chunk].wait_recv()
            at = w_rows(g_rank, chunk)
            held = wo.at[lax.rem(x - k + nx, nx), at, :]
            for j in range(1, ng):
                copy = remote(held, held, ys.at[k, chunk, j], yr.at[k, chunk, j], y_peer(j))
                copy.start()
                y_copies.append(copy)

    q_copies = []
    for i in (1, 0, 2):
        loads[i].wait()

        def project(g, i=i):
            at = pl.ds(pl.multiple_of(g * block, block), block)
            made = jnp.dot(xn[at, :], wqkv[i], preferred_element_type=f32).astype(bf16)
            for r in range(group):
                for p in range(pairs):
                    piece = made[r * frames : (r + 1) * frames, p * LANES : (p + 1) * LANES]
                    qkv_s[(g * group + r) * pairs + p, i] = piece

        loop(recs // group, project)
        for k in range(1, n):
            dest = ctx_at(k)
            copy = remote(
                qkv_s.at[lax.rem(dest, units), i], qkv_r.at[c, i], qs.at[i, k], qr.at[i, k], {"ctx": dest}
            )
            when(has_unit(dest))(copy.start)
            q_copies.append((copy, dest, i))

        @when(has_unit(c))
        def _(i=i):
            qkv_r[c, i] = qkv_s[lax.rem(c, units), i]

    z_copies = [
        remote(atto.at[k], att_all.at[x, lax.rem(c, units)], zs.at[k], zr.at[k], {"ctx": ctx_at(k)})
        for k in range(1, n)
    ]

    for copy in w_copies.values():
        copy.start()
    for i in (5, 3, 4):
        loads[i].start()
    smalls[2].wait()

    def arrived(which):
        @when(has_unit(c))
        def _():
            for copy, _dest, i in q_copies:
                if i in which:
                    copy.wait_recv()

    arrived((1, 0))
    own_rec = lax.div(lax.rem(c, units), pairs)
    live_keys = counts[own_rec]
    key_count = n * frames
    lane = lax.broadcasted_iota(jnp.int32, (1, LANES), 1)
    low = lane < HEAD_DIM
    seen = lax.broadcasted_iota(jnp.int32, (1, key_count), 1) < live_keys
    slots = w_s.shape[0]

    def weigh(k0, slot):
        keys = qkv_r[:, 1].reshape(key_count, LANES)
        queries = jnp.concatenate([qkv_r[ctx_at(k0), 0], qkv_r[ctx_at(k0 + 1), 0]], axis=0)
        for h in range(2):
            mine = jnp.where(low if h == 0 else jnp.logical_not(low), queries, jnp.zeros((), bf16))
            scores = lax.dot_general(mine, keys, (((1,), (1,)), ((), ())), preferred_element_type=f32)
            scores = jnp.where(seen, scores, masked_score)
            top = jnp.max(scores, axis=-1, keepdims=True)
            weights = jnp.exp((scores - top) * (HEAD_DIM**-0.5))
            tot_s[slot, h] = jnp.sum(weights, axis=-1, keepdims=True)
            w_s[slot, h] = weights.astype(bf16)

    def mix(k0, slot):
        values = qkv_r[:, 2].reshape(key_count, LANES)
        heads = [
            jnp.dot(w_s[slot, h], values, preferred_element_type=f32) / tot_s[slot, h] for h in range(2)
        ]
        both = jnp.where(low, heads[0], heads[1]).astype(bf16)
        atto[k0] = both[:frames]
        atto[k0 + 1] = both[frames:]

    def give(k):
        if k == 0:
            att_all[x, lax.rem(c, units)] = atto[0]
        else:
            z_copies[k - 1].start()

    starts = list(range(0, n, 2))
    if slots > 1:
        @when(has_unit(c))
        def _():
            for slot, k0 in enumerate(starts):
                weigh(k0, slot)

    hand_on(0)
    hand_on(1)
    arrived((2,))

    @when(has_unit(c))
    def _():
        if slots > 1:
            for slot, k0 in reversed(list(enumerate(starts))):
                mix(k0, slot)
                give(k0 + 1)
                give(k0)
        else:
            def whole_step(i, carry):
                weigh(2 * i, 0)
                mix(2 * i, 0)
                return carry

            lax.fori_loop(0, n // 2, whole_step, 0)
            for k in range(n):
                give(k)

    for chunk in range(2, W_CHUNKS):
        hand_on(chunk)

    f_copies = []
    for k in [0] + list(range(n - 1, 0, -1)):
        unit = lax.rem(c - k + n, n)
        spot = lax.rem(unit, units)

        @when(has_unit(unit))
        def _(k=k, unit=unit, spot=spot):
            if k > 0:
                remote(atto.at[k], att_all.at[x, spot], zs.at[k], zr.at[k], {"ctx": unit}).wait_recv()
            for j in range(1, nx):
                remote(
                    att_all.at[x, spot], att_all.at[x, spot], fs.at[j, k], fr.at[j, k], x_peer(j)
                ).start()

        for j in range(1, nx):
            f_copies.append(
                (remote(att_all.at[x, spot], att_all.at[x, spot], fs.at[j, k], fr.at[j, k], x_peer(j)), unit)
            )

    loads[5].wait()
    for copy in y_copies:
        copy.wait_recv()
    for copy, unit in f_copies:
        when(has_unit(unit))(copy.wait_recv)

    s_copies = []
    for rec in range(recs):
        gathered = jnp.concatenate(
            [att_all[i, rec * pairs + p] for i in range(nx) for p in range(pairs)], axis=1
        )
        parts[rec] = jnp.dot(
            gathered, wo[...].reshape(nx * pairs * LANES, width), preferred_element_type=f32
        ).astype(bf16)
        copy = remote(parts.at[rec], sibs.at[rec], ss.at[rec], sr.at[rec], sibling)
        copy.start()
        s_copies.append(copy)

    smalls[3].wait()
    conv_gain = cg[...].reshape(1, width)
    for rec in range(recs):
        s_copies[rec].wait_recv()

        def norm_conv(i, rec=rec):
            near = pl.ds(pl.multiple_of(i * 32, 32), 32)
            at = pl.ds(pl.multiple_of(rec * frames + i * 32, 32), 32)
            total = feat[at, :].astype(f32) + (parts[rec, near, :].astype(f32) + sibs[rec, near, :].astype(f32))
            res[at, :] = total
            xn[at, :] = normalise(total, conv_gain)

        lax.fori_loop(0, frames // 32, lambda i, carry: (norm_conv(i), carry)[1], 0, unroll=4)

    loads[3].wait()
    first_frame = c * frames
    frame_ids = first_frame + lax.broadcasted_iota(jnp.int32, (frames, 1), 0)

    def gate(g):
        at = pl.ds(pl.multiple_of(g * block, block), block)
        value_half = jnp.dot(xn[at, :], wglu[0], preferred_element_type=f32)
        gate_half = jnp.dot(xn[at, :], wglu[1], preferred_element_type=f32)
        gated = value_half * jax.nn.sigmoid(gate_half)
        for r in range(group):
            rec = g * group + r
            kept = jnp.where(frame_ids < counts[rec], gated[r * frames : (r + 1) * frames], 0.0).astype(bf16)
            gb[rec] = kept
            gp[rec, RIM : RIM + frames, :] = kept.astype(f32)

    loop(recs // group, gate)

    def up():
        return remote(gb.at[:, frames - RIM : frames, :], halo.at[0], hs.at[0], hr.at[0], {"ctx": lax.rem(c + 1, n)})

    def down():
        return remote(gb.at[:, 0:RIM, :], halo.at[1], hs.at[1], hr.at[1], {"ctx": lax.rem(c + n - 1, n)})

    @pl.when(c < n - 1)
    def _():
        up().start()

    @pl.when(c > 0)
    def _():
        down().start()

    for copy in smalls[4:]:
        copy.wait()
    bound = clip[...].astype(f32) / 16.0
    least[...] = -bound
    most[...] = bound
    scale = bns[...].reshape(1, chans)
    shift = bnb[...].reshape(1, chans)

    def depthwise(rec, start, count):
        for lo in range(0, chans, LANES):
            hi = min(lo + LANES, chans)
            total = jnp.zeros((count, hi - lo), f32)
            for tap in range(taps):
                begin = start + tap + RIM - taps // 2
                total = total + gp[rec, begin : begin + count, lo:hi] * ker[tap : tap + 1, lo:hi]
            v = total * scale[:, lo:hi] + shift[:, lo:hi]
            act[rec, start : start + count, lo:hi] = (v * jax.nn.sigmoid(v)).astype(bf16)

    def rim():
        @pl.when(c > 0)
        def _():
            up().wait_recv()

        @pl.when(c == 0)
        def _():
            halo[0] = jnp.zeros(halo.shape[1:], bf16)

        @pl.when(c < n - 1)
        def _():
            down().wait_recv()

        @pl.when(c == n - 1)
        def _():
            halo[1] = jnp.zeros(halo.shape[1:], bf16)

    b_copies = []
    e_copies = []

    def pass_on(rec):
        b_copies[rec].wait_recv()
        for i in range(nx):
            sum5[rec, i] = (p5[rec, i, core].astype(f32) + s5[rec, i].astype(f32)).astype(bf16)
        for k in range(1, nx):
            copy = remote(sum5.at[rec, lax.rem(x + k, nx)], x5.at[rec, k], es.at[rec, k], er.at[rec, k], x_peer(k))
            copy.start()
            e_copies.append(copy)

    for rec in range(recs):
        if rec == 0:
            depthwise(rec, RIM, frames - 2 * RIM)
            rim()
            loads[4].wait()
        gp[rec, 0:RIM, :] = halo[0, rec].astype(f32)
        gp[rec, RIM + frames : 2 * RIM + frames, :] = halo[1, rec].astype(f32)
        if rec == 0:
            depthwise(rec, 0, RIM)
            depthwise(rec, frames - RIM, RIM)
        else:
            depthwise(rec, 0, frames // 2)
            pass_on(rec - 1)
            depthwise(rec, frames // 2, frames // 2)
        made = jnp.dot(act[rec], wpw[...], preferred_element_type=f32)
        p5[rec] = made.reshape(nx, 2, rm, width).astype(bf16)
        copy = remote(p5.at[rec, :, 1 - core], s5.at[rec], bs.at[rec], br.at[rec], sibling)
        copy.start()
        b_copies.append(copy)
    pass_on(recs - 1)

    row_start = pl.multiple_of(m * rm, rm)
    mine_ids = first_frame + row_start + lax.broadcasted_iota(jnp.int32, (rm, 1), 0)
    for rec in range(recs):
        for k in range(1, nx):
            e_copies[rec * (nx - 1) + k - 1].wait_recv()
        at = pl.ds(pl.multiple_of(rec * frames + row_start, rm), rm)
        total = res[at, :] + sum5[rec, x].astype(f32)
        for k in range(1, nx):
            total = total + x5[rec, k].astype(f32)
        out[rec] = jnp.where(mine_ids < counts[rec], total, 0.0).astype(bf16)

    for copy, dest, _i in q_copies:
        when(has_unit(dest))(copy.wait_send)

    @when(has_unit(c))
    def _():
        for copy in z_copies:
            copy.wait_send()

    for copy, unit in f_copies:
        when(has_unit(unit))(copy.wait_send)
    for copy in list(w_copies.values()) + y_copies + s_copies + b_copies + e_copies:
        copy.wait_send()

    @pl.when(c < n - 1)
    def _():
        up().wait_send()

    @pl.when(c > 0)
    def _():
        down().wait_send()


def shards(n, mp, ng, features, frame_counts, attn_gain, w_qkv, w_out, conv_gain, w_glu, kernel, bn_scale, bn_shift, w_pw, clip_level):
    recs, frames, width = features.shape
    nx = mp // 2
    rows = recs * frames
    local = w_qkv.shape[2]
    units = recs * local // LANES
    chans = w_glu.shape[2]
    rm = frames // mp
    taps = kernel.shape[0]
    vmem = pl.BlockSpec(memory_space=pltpu.VMEM)
    hbm = pl.BlockSpec(memory_space=pl.ANY)
    dma = pltpu.SemaphoreType.DMA
    slots = n // 2 if n <= 4 else 1
    scratch = [
        pltpu.VMEM((rows, width), bf16),
        pltpu.SMEM(frame_counts.shape, jnp.int32),
        pltpu.VMEM(attn_gain.shape, f32),
        pltpu.VMEM(conv_gain.shape, f32),
        pltpu.VMEM(kernel.shape, f32),
        pltpu.VMEM(bn_scale.shape, f32),
        pltpu.VMEM(bn_shift.shape, f32),
        pltpu.VMEM(clip_level.shape, jnp.int32),
        pltpu.VMEM(w_qkv.shape, bf16),
        pltpu.VMEM((nx, local, width), bf16),
        pltpu.VMEM(w_glu.shape, bf16),
        pltpu.VMEM(w_pw.shape, bf16),
        pltpu.VMEM((rows, width), bf16),
        pltpu.VMEM((units, 3, frames, LANES), bf16),
        pltpu.VMEM((n, 3, frames, LANES), bf16),
        pltpu.VMEM((n, frames, LANES), bf16),
        pltpu.VMEM((nx, units, frames, LANES), bf16),
        pltpu.VMEM((slots, 2, 2 * frames, n * frames), bf16),
        pltpu.VMEM((slots, 2, 2 * frames, 1), f32),
        pltpu.VMEM((recs, frames, width), bf16),
        pltpu.VMEM((recs, frames, width), bf16),
        pltpu.VMEM((rows, width), f32),
        pltpu.VMEM((recs, frames, chans), bf16),
        pltpu.VMEM((recs, frames + 2 * RIM, chans), f32),
        pltpu.VMEM((2, recs, RIM, chans), bf16),
        pltpu.VMEM((recs, frames, chans), bf16),
        pltpu.VMEM((recs, nx, 2, rm, width), bf16),
        pltpu.VMEM((recs, nx, rm, width), bf16),
        pltpu.VMEM((recs, nx, rm, width), bf16),
        pltpu.VMEM((recs, nx, rm, width), bf16),
        dma((6,)),
        dma((8,)),
        dma((3, n)), dma((3, n)),
        dma((nx, W_CHUNKS)), dma((nx, W_CHUNKS)),
        dma((nx, W_CHUNKS, ng)), dma((nx, W_CHUNKS, ng)),
        dma((n,)), dma((n,)),
        dma((nx, n)), dma((nx, n)),
        dma((recs,)), dma((recs,)),
        dma((2,)), dma((2,)),
        dma((recs,)), dma((recs,)),
        dma((recs, nx)), dma((recs, nx)),
    ]
    summed, least, most = pl.pallas_call(
        functools.partial(fused, n, nx, ng, recs, frames, taps),
        out_shape=(
            jax.ShapeDtypeStruct((recs, rm, width), bf16),
            jax.ShapeDtypeStruct((width,), f32),
            jax.ShapeDtypeStruct((width,), f32),
        ),
        in_specs=[hbm] * 12,
        out_specs=(vmem, vmem, vmem),
        scratch_shapes=scratch,
        compiler_params=pltpu.CompilerParams(
            collective_id=0, has_side_effects=True, vmem_limit_bytes=56 * 2**20
        ),
    )(
        features.reshape(rows, width), frame_counts, attn_gain, w_qkv, w_out, conv_gain, w_glu, kernel,
        bn_scale, bn_shift, w_pw, clip_level,
    )
    return jnp.clip(summed.astype(f32), least, most).astype(bf16)


def solution(mesh):
    return jax.shard_map(
        functools.partial(shards, mesh.shape["ctx"], mesh.shape["mp"], mesh.shape["groups"]),
        mesh=mesh,
        in_specs=(
            P("groups", "ctx", None),
            P("groups"),
            P(),
            P(None, None, "mp"),
            P("mp", None),
            P(),
            P(None, None, "mp"),
            P(None, "mp"),
            P("mp"),
            P("mp"),
            P("mp", None),
            P(),
        ),
        out_specs=P("groups", ("ctx", "mp"), None),
        check_vma=False,
    )
```
